256 devices in a mesh: sky: 16 (over x, y), epoch: 16 (over z, core).
Axes of the slice: x: 4, y: 4, z: 8, core: 2. Of those that a mesh axis runs over, the one named last changes fastest.
Arguments:
- params: bfloat16 [2048, 64], P('sky'), may hold values from -6 to 6
- basis: bfloat16 [64, 4096], replicated, may hold values from -0.75 to 0.75
- psf_taps: float32 [16, 2, 51], P('epoch'), may hold values from 0.02 to 1
- send_index: int32 [16, 16, 16], P('sky'), may hold values from 0 to 127
- tile_count: int32 [16, 16], P('sky'), may hold values from 0 to 16, as said below
- stamp_row: int32 [16, 16, 16], P('sky'), may hold values from 0 to 256
- stamp_col: int32 [16, 16, 16], P('sky'), may hold values from 0 to 448
- observed: float32 [16, 4096, 512], P('epoch', 'sky'), may hold values from 0 to 6
- background: float32 [16, 4096, 512], P('epoch', 'sky'), may hold values from 0.5 to 2
Outputs:
- param_grad: float32 [2048, 64], P('sky')
- residual: float32 [16, 4096, 512], P('epoch', 'sky')
The draws below stay inside these ranges and needn't reach their ends.
Inputs may be any that keep to these rules, and one draw needn't show every extreme that they name: `send_index`: slots with k >= tile_count[t, o] are dead and may name any row; they still lie within range. `tile_count`: some tiles are crowded and receive nearly 16 slots from every owner; in every draw at least one tile receives exactly 16 from owner 0. `stamp_row`: A stamp lies inside its tile's canvas.
All inputs are finite; a program needn't handle non-finite values.
Results may differ from the reference program's by a relative error of at most 0.0003.
Values may be sent and summed in bfloat16 or wider, within the bound.
No kernel may reach another device: no remote copies, remote signals or barrier semaphores. Data moves between devices by JAX's collectives and lax.ppermute only.
A program may use at most 64 MiB of HBM per device.

```python
import math
import jax
import jax.numpy as jnp
from jax import lax

P_SIZE = 64
STAMP = 64
TAPS = 51
TR = 256
TW = 512
SRC_DEV = 128
CAP = 16
MARGIN = 32
CANVAS = 320
NROWS = 4096
SOURCES = 2048
N_SKY = 16
N_EPOCH = 16


def draw_tile_count(key, part):
    key_one, key_two, key_three, key_four = jax.random.split(jax.random.fold_in(key, 17), 4)
    crowded = jax.random.randint(key_one, (N_SKY,), 0, 4) == 0
    chosen = jax.random.randint(key_two, (), 0, N_SKY)
    crowded = crowded | (jnp.arange(N_SKY) == chosen)
    light = jax.random.randint(key_three, (N_SKY, N_SKY), 0, CAP // 2 + 1)
    heavy = CAP - jax.random.randint(key_four, (N_SKY, N_SKY), 0, CAP // 4 + 1)
    count = jnp.where(crowded[:, None], heavy, light)
    first_owner = jnp.arange(N_SKY)[None, :] == 0
    count = jnp.where(crowded[:, None] & first_owner, CAP, count)
    return count.astype(jnp.int32)


def plant(drawn, rng, least, high):
    spot = [jax.random.randint(jax.random.fold_in(rng, axis), (), 0, length) for axis, length in enumerate(drawn.shape)]
    main_axis = drawn.shape.index(max(drawn.shape))
    next_to = spot[:main_axis] + [(spot[main_axis] + 1) % drawn.shape[main_axis]] + spot[main_axis + 1:]
    return drawn.at[tuple(spot)].set(least).at[tuple(next_to)].set(high)


def block_scale(key, extent, cuts, least, top_value):
    def one(position, blocks):
        steps = jax.random.uniform(jax.random.fold_in(jax.random.fold_in(key, 6), position), (blocks,), jnp.float32, least / len(cuts), top_value / len(cuts))
        return jnp.repeat(jnp.exp(steps), extent[position] // blocks).reshape((-1,) + (1,) * (len(extent) - position - 1))

    loudness = one(*cuts[0])
    for cut in cuts[1:]:
        loudness = loudness * one(*cut)
    return loudness


def centred(rng, dims, deviation, most, pieces=(), kind=jnp.bfloat16):
    drawn = jax.random.normal(rng, dims, jnp.float32) * deviation
    if len(pieces) > 0:
        drawn = block_scale(rng, dims, pieces, -0.22, 0.18) * drawn
    return jnp.clip(drawn, min=-most, max=most).astype(kind)


def setup_inputs(seed: int = 0) -> dict:
    streams_of = jax.random.split(jax.random.key(seed), 10)
    return {
        "params": centred(streams_of[0], (SOURCES, P_SIZE), 1.0, 6.0, ((0, 16),)),
        "basis": centred(streams_of[1], (P_SIZE, STAMP * STAMP), P_SIZE ** -0.5, 0.75),
        "psf_taps": jnp.clip(jnp.exp(math.log(1.0) - 3.912023 * jax.random.uniform(streams_of[2], (N_EPOCH, 2, TAPS), jnp.float32) ** block_scale(streams_of[2], (N_EPOCH, 2, TAPS), ((0, 16),), -0.2, 0.2)), 0.02, 1.0),
        "send_index": plant(jax.random.randint(streams_of[3], (N_SKY, N_SKY, CAP), 0, SRC_DEV), jax.random.fold_in(streams_of[3], 1), 0, SRC_DEV - 1).astype(jnp.int32),
        "tile_count": draw_tile_count(jax.random.fold_in(streams_of[9], 71), 0),
        "stamp_row": plant(jax.random.randint(streams_of[5], (N_SKY, N_SKY, CAP), 0, CANVAS - STAMP + 1), jax.random.fold_in(streams_of[5], 1), 0, CANVAS - STAMP).astype(jnp.int32),
        "stamp_col": plant(jax.random.randint(streams_of[6], (N_SKY, N_SKY, CAP), 0, TW - STAMP + 1), jax.random.fold_in(streams_of[6], 1), 0, TW - STAMP).astype(jnp.int32),
        "observed": jnp.clip(6.0 * jax.random.uniform(streams_of[7], (N_EPOCH, NROWS, TW), jnp.float32) ** block_scale(streams_of[7], (N_EPOCH, NROWS, TW), ((0, 16), (1, 16)), -0.2, 0.2), 0.0, 6.0),
        "background": jnp.clip(jnp.exp(math.log(2.0) - 1.3862944 * jax.random.uniform(streams_of[8], (N_EPOCH, NROWS, TW), jnp.float32) ** block_scale(streams_of[8], (N_EPOCH, NROWS, TW), ((0, 16), (1, 16)), -0.2, 0.2)), 0.5, 2.0),
    }


def toeplitz(taps, width):
    half = (taps.shape[0] - 1) // 2
    rows_at = jnp.arange(width, dtype=jnp.int32)[:, None]
    cols_at = jnp.arange(width, dtype=jnp.int32)[None, :]
    where_at = rows_at - cols_at + half
    inside = (where_at >= 0) & (where_at < taps.shape[0])
    return jnp.where(inside, taps[jnp.clip(where_at, 0, taps.shape[0] - 1)], jnp.zeros((), taps.dtype))


def reference(params, basis, psf_taps, send_index, tile_count, stamp_row, stamp_col, observed, background):
    highest = lax.Precision.HIGHEST
    owners = jnp.arange(N_SKY, dtype=jnp.int32)
    global_rows = send_index + (owners * SRC_DEV)[:, None, None]
    dest_rows = jnp.transpose(global_rows, (1, 0, 2)).reshape(N_SKY, -1)
    slot_params = params[dest_rows]
    live = (jnp.arange(CAP, dtype=jnp.int32)[None, None, :] < tile_count[:, :, None]).astype(jnp.float32)
    live = live.reshape(N_SKY, -1)
    intrinsic = jnp.dot(slot_params.reshape(-1, P_SIZE), basis, preferred_element_type=jnp.float32)
    intrinsic = intrinsic.reshape(N_SKY, -1, STAMP, STAMP)
    taps = psf_taps / jnp.sum(psf_taps, axis=-1, keepdims=True)
    row_pos = stamp_row.reshape(N_SKY, -1)
    col_pos = stamp_col.reshape(N_SKY, -1)
    stamp_span = jnp.arange(STAMP, dtype=jnp.int32)
    basis_wide = basis.astype(jnp.float32).T

    def exposure(total, inputs):
        taps_e, obs_e, back_e = inputs
        row_kernel = toeplitz(taps_e[0], STAMP)
        col_kernel = toeplitz(taps_e[1], STAMP)

        def indices(rows_t, cols_t):
            count = rows_t.shape[0]
            rows_full = jnp.broadcast_to(rows_t[:, None, None] + stamp_span[None, :, None], (count, STAMP, STAMP))
            cols_full = jnp.broadcast_to(cols_t[:, None, None] + stamp_span[None, None, :], (count, STAMP, STAMP))
            return rows_full, cols_full

        def render_tile(args):
            intr_t, live_t, rows_t, cols_t = args
            rendered = jnp.einsum('ab,nbc,dc->nad', row_kernel, intr_t, col_kernel, precision=highest)
            rendered = rendered * live_t[:, None, None]
            stamps = lax.optimization_barrier(rendered.astype(jnp.bfloat16)).astype(jnp.float32)
            rows_full, cols_full = indices(rows_t, cols_t)
            return jnp.zeros((CANVAS, TW), jnp.float32).at[rows_full, cols_full].add(stamps)

        canvas = lax.map(render_tile, (intrinsic, live, row_pos, col_pos))
        core = canvas[:, MARGIN:MARGIN + TR]
        below = jnp.concatenate([jnp.zeros((1, MARGIN, TW), jnp.float32), canvas[:-1, MARGIN + TR:]], axis=0)
        above = jnp.concatenate([canvas[1:, :MARGIN], jnp.zeros((1, MARGIN, TW), jnp.float32)], axis=0)
        core = core.at[:, :MARGIN].add(below).at[:, TR - MARGIN:].add(above)
        image = core.reshape(NROWS, TW)
        model = back_e + jax.nn.softplus(image)
        residual = (obs_e / model - 1.0) * jax.nn.sigmoid(image)
        padded = jnp.pad(residual.astype(jnp.bfloat16), ((MARGIN, MARGIN), (0, 0)))

        def adjoint_tile(args):
            tile, live_t, rows_t, cols_t = args
            reach = lax.dynamic_slice_in_dim(padded, (tile * TR).astype(jnp.int32), CANVAS, 0)
            rows_full, cols_full = indices(rows_t, cols_t)
            window = reach[rows_full, cols_full].astype(jnp.float32)
            pulled = jnp.einsum('ba,nbc,cd->nad', row_kernel, window, col_kernel, precision=highest)
            pulled = pulled * live_t[:, None, None]
            return jnp.dot(pulled.reshape(-1, STAMP * STAMP), basis_wide, precision=highest)

        grads = lax.map(adjoint_tile, (owners, live, row_pos, col_pos))
        return total + grads, residual

    start = jnp.zeros((N_SKY, N_SKY * CAP, P_SIZE), jnp.float32)
    total, residual = lax.scan(exposure, start, (taps, observed, background))
    param_grad = jnp.zeros((SOURCES, P_SIZE), jnp.float32).at[dest_rows.reshape(-1)].add(total.reshape(-1, P_SIZE))
    return param_grad, residual
```

```python
import functools
import math

import jax
import jax.numpy as jnp
from jax import lax
from jax.experimental import pallas as pl
from jax.experimental.pallas import tpu as pltpu
from jax.sharding import PartitionSpec as P

PS = 64
ST = 64
TAPS = 51
HALF = 25
TR = 256
TW = 512
MARGIN = 32
CANVAS = 320
CAP = 16
NSKY = 16
SLOTS = 768
SROWS = 776
OFF = 64
CROWS = 448
XROWS = 320
NCANV = 4
GROUP = 8
CHUNKS = 16
HIGHEST = lax.Precision.HIGHEST


def dot(a, b, dims, precision=None):
    return lax.dot_general(a, b, (dims, ((), ())), precision=precision, preferred_element_type=jnp.float32)


def split3(x):
    high = x.astype(jnp.bfloat16)
    rest = x - high.astype(jnp.float32)
    mid = rest.astype(jnp.bfloat16)
    low = (rest - mid.astype(jnp.float32)).astype(jnp.bfloat16)
    return high, mid, low


def iota(shape, axis):
    return lax.broadcasted_iota(jnp.int32, shape, axis)


def basis_kernel(taps_s, taps_v, basis_ref, out_ref, xs, ts):
    f32 = jnp.float32
    total = jnp.sum(taps_v[...], axis=1, keepdims=True)
    at = iota((128, 32), 0)
    where_at = at % 64 - (2 * iota((128, 32), 1) + at // 64) + HALF
    row_k = jnp.zeros((128, 32), f32)
    for t in range(TAPS):
        row_k = jnp.where(where_at == t, taps_s[0, t], row_k)
    row_k = row_k / total[0:1, :]
    row_parts = jnp.concatenate(split3(row_k), axis=1)
    b_at, d_at = iota((64, 256), 0), iota((64, 256), 1)
    where_at = d_at % 64 - b_at + HALF
    col_k = jnp.zeros((64, 256), f32)
    for t in range(TAPS):
        col_k = jnp.where(where_at == t, taps_s[1, t], col_k)
    col_k = col_k / total[1:2, :]
    col_k = jnp.concatenate([jnp.where(d_at // 64 == i, col_k, 0.0) for i in range(4)], axis=0)
    col_h, col_m, col_l = split3(col_k)

    for j in range(32):
        xs[j * 64:(j + 1) * 64, :] = basis_ref[:, j * 128:(j + 1) * 128].astype(f32)
    lane = iota((64, 128), 1)

    def rows_step(g, unused):
        images = [xs[pl.ds(g * 8 + i, 32, stride=64), :].astype(jnp.bfloat16) for i in range(8)]
        wide = jnp.concatenate(images, axis=1)
        made = dot(row_parts, jnp.concatenate([wide, wide, wide], axis=0), ((1,), (0,)))
        for i in range(8):
            both = jnp.where(lane < 64, made[:64, i * 128:(i + 1) * 128], made[64:, i * 128:(i + 1) * 128])
            both = both + pltpu.roll(both, 64, 1)
            ts[pl.ds(g * 8 + i, 32, stride=64), :] = jnp.where(lane[:32] < 64, both[:32], both[32:])
        return unused

    lax.fori_loop(0, 8, rows_step, 0)

    def cols_step(c, unused):
        base = pl.multiple_of(c * 128, 128)
        x = jnp.concatenate([ts[pl.ds(base, 64), :], ts[pl.ds(base + 64, 64), :]], axis=1)
        xh, xm, xl = split3(x)
        d = functools.partial(dot, dims=((1,), (0,)))
        y = d(xl, col_h) + d(xh, col_l) + d(xm, col_m) + d(xm, col_h) + d(xh, col_m) + d(xh, col_h)
        yh, ym, yl = split3(y)
        out_ref[c, 0:64, :] = yh
        out_ref[c, 64:128, :] = ym
        out_ref[c, 128:192, :] = yl
        return unused

    lax.fori_loop(0, CHUNKS, cols_step, 0)


def sky_kernel(own_s, up_s, down_s, b_ref, sp_ref, obs_ref, back_ref, halo_up_ref, halo_down_ref,
               res_ref, keep_ref, give_ref, ss, xs, acc, listed, *canvases):
    f32 = jnp.float32
    tile = lax.axis_index("sky")
    core = lax.axis_index("epoch") % 2
    lane8 = iota((8, 128), 1)

    zero = jnp.zeros((CROWS, 128), f32)
    for canvas in canvases:
        for q in range(5):
            canvas[q * CROWS:(q + 1) * CROWS, :] = zero
    for j in range(32):
        ss[j * SROWS + SLOTS:(j + 1) * SROWS, :] = jnp.zeros((SROWS - SLOTS, 128), f32)

    sp = sp_ref[...]
    sp3 = jnp.concatenate([sp, sp, sp], axis=1)

    def render(c, count):
        made = dot(sp3, b_ref[c], ((1,), (0,)))
        made = made.astype(jnp.bfloat16).astype(f32)
        base = pl.multiple_of(c * (2 * SROWS), 8)
        ss[pl.ds(base, SLOTS), :] = made[:, :128]
        ss[pl.ds(base + SROWS, SLOTS), :] = made[:, 128:]
        for which, ref in enumerate((up_s, own_s, down_s)):
            total = ref[32, c]
            for k in range(CAP):
                row, col = ref[c, k], ref[16 + c, k]
                live = k < total
                if which == 0:
                    live = live & (row > 192)
                if which == 2:
                    live = live & (row < 64)
                where_to = row + (which - 1) * TR + OFF
                listed[count] = ((c * 48 + which * 16 + k) * 512 + where_to) * 512 + col
                count = count + live.astype(jnp.int32)
        return count

    count = lax.fori_loop(0, CHUNKS, render, jnp.int32(0))
    for i in range(GROUP):
        listed[count + i] = (SLOTS * 512 + OFF) * 512

    lane32 = iota((32, 128), 1)

    def place(g, unused):
        for i in range(GROUP):
            canvas = canvases[i % NCANV]
            entry = listed[g * GROUP + i]
            slot = entry >> 18
            row = (entry >> 9) & 511
            col = entry & 511
            shift = col & 127
            start = (col >> 7) * CROWS + row
            stamp = ss[pl.ds(slot, 32, stride=SROWS), :]
            first = (lane32 >= shift) & (lane32 < shift + 64)
            second = lane32 < shift - 64
            for h in range(2):
                turned = pltpu.roll(stamp, (shift + 64 * h) & 127, 1)
                a = start + 32 * h
                canvas[pl.ds(a, 32), :] += jnp.where(first, turned, 0.0)
                canvas[pl.ds(a + CROWS, 32), :] += jnp.where(second, turned, 0.0)
        return unused

    lax.fori_loop(0, (count + GROUP - 1) // GROUP, place, 0)

    def pixels(observed, background, image):
        e = jnp.exp(-jnp.abs(image))
        soft = jnp.maximum(image, 0.0) + jnp.log1p(e)
        sig = jnp.where(image >= 0.0, 1.0, e) / (1.0 + e)
        return (observed / (background + soft) - 1.0) * sig

    def image_at(q, row, rows):
        at = pl.ds(q * CROWS + OFF + row, rows)
        image = canvases[0][at, :]
        for canvas in canvases[1:]:
            image = image + canvas[at, :]
        return image

    def rounded(x):
        return x.astype(jnp.bfloat16).astype(f32)

    for q in range(4):
        lanes = slice(q * 128, (q + 1) * 128)
        r = pixels(halo_up_ref[:32, lanes], halo_up_ref[32:, lanes], image_at(q, 0, 32))
        xs[q * XROWS:q * XROWS + 32, :] = jnp.where(tile > 0, rounded(r), 0.0)
        r = pixels(halo_down_ref[:32, lanes], halo_down_ref[32:, lanes], image_at(q, 288, 32))
        xs[q * XROWS + 288:q * XROWS + 320, :] = jnp.where(tile < NSKY - 1, rounded(r), 0.0)

    def block(i, unused):
        base = pl.multiple_of(i * 32, 32)
        for q in range(4):
            lanes = slice(q * 128, (q + 1) * 128)
            r = pixels(obs_ref[pl.ds(base, 32), lanes], back_ref[pl.ds(base, 32), lanes], image_at(q, 32 + base, 32))
            res_ref[pl.ds(base, 32), lanes] = r
            xs[pl.ds(q * XROWS + 32 + base, 32), :] = rounded(r)
        return unused

    lax.fori_loop(0, 8, block, 0)

    def window(g, unused):
        for i in range(GROUP):
            o = g // 2
            k = (g % 2) * GROUP + i
            slot = g * GROUP + i
            row, col = own_s[o, k], own_s[16 + o, k]
            shift = col & 127
            start = (col >> 7) * XROWS + row
            parts = []
            for h in range(2):
                a = start + 32 * h
                seen = jnp.where(lane32 >= shift, xs[pl.ds(a, 32), :], xs[pl.ds(a + XROWS, 32), :])
                parts.append(pltpu.roll(seen, (64 * h - shift) & 127, 1))
            ss[pl.ds(slot, 32, stride=SROWS), :] = jnp.where(lane32 < 64, parts[0], parts[1])
        return unused

    lax.fori_loop(0, 256 // GROUP, window, 0)

    def gather(c, total):
        base = pl.multiple_of(c * (2 * SROWS), 8)
        w = jnp.concatenate([ss[pl.ds(base, 256), :], ss[pl.ds(base + SROWS, 256), :]], axis=1).astype(jnp.bfloat16)
        return total + dot(w, b_ref[c], ((1,), (1,)))

    total = lax.fori_loop(0, CHUNKS, gather, jnp.zeros((256, 192), f32))
    grad = total[:, 128:192] + total[:, 64:128] + total[:, :64]
    slot_k = iota((CAP, 64), 0)
    for o in range(NSKY):
        acc[o * 16:(o + 1) * 16, :] = jnp.where(slot_k < own_s[32, o], grad[o * 16:(o + 1) * 16], 0.0)
    for o in range(NSKY):
        keep_ref[o * 8:(o + 1) * 8, :] = acc[pl.ds(pl.multiple_of(o * 16 + core * 8, 8), 8), :]
        give_ref[o * 8:(o + 1) * 8, :] = acc[pl.ds(pl.multiple_of(o * 16 + 8 - core * 8, 8), 8), :]


def owner_kernel(index_s, got_ref, out_ref, hot):
    f32 = jnp.float32
    core = lax.axis_index("epoch") % 2
    lane = iota((1, 128), 1)
    for t in range(NSKY):
        for k in range(8):
            hot[t * 8 + k:t * 8 + k + 1, :] = jnp.where(lane == index_s[t, core * 8 + k], 1.0, 0.0).astype(f32)
    sums = []
    for t in range(NSKY):
        s = got_ref[t * 8]
        for z in range(1, 8):
            s = s + got_ref[t * 8 + z]
        sums.append(s)
    out_ref[...] = dot(hot[...], jnp.concatenate(sums, axis=0), ((0,), (0,)), HIGHEST)


SM = pl.BlockSpec(memory_space=pltpu.SMEM)
VM = pl.BlockSpec(memory_space=pltpu.VMEM)


def on_device(params, basis, psf_taps, send_index, tile_count, stamp_row, stamp_col, observed, background):
    f32 = jnp.float32
    n = NSKY
    index = send_index[0]
    spread = jnp.concatenate([jnp.roll(index, 1, 0), index, jnp.roll(index, -1, 0)], axis=1)
    outgoing = params[spread]
    slot_params = lax.all_to_all(outgoing, "sky", split_axis=0, concat_axis=0, tiled=True).reshape(SLOTS, PS)

    to_next = [(i, i + 1) for i in range(n - 1)]
    to_prev = [(i + 1, i) for i in range(n - 1)]
    spots = jnp.concatenate([stamp_row[0], stamp_col[0], tile_count], axis=0)
    obs, back = observed[0], background[0]
    spots_up = lax.ppermute(spots, "sky", to_next)
    spots_down = lax.ppermute(spots, "sky", to_prev)
    halo_up = lax.ppermute(jnp.concatenate([obs[TR - 32:], back[TR - 32:]], axis=0), "sky", to_next)
    halo_down = lax.ppermute(jnp.concatenate([obs[:32], back[:32]], axis=0), "sky", to_prev)

    taps = psf_taps[0]
    shaped = pl.pallas_call(
        basis_kernel,
        out_shape=jax.ShapeDtypeStruct((CHUNKS, 192, 256), jnp.bfloat16),
        in_specs=[SM, VM, VM],
        out_specs=VM,
        scratch_shapes=[pltpu.VMEM((2048, 128), f32), pltpu.VMEM((2048, 128), f32)],
        compiler_params=pltpu.CompilerParams(vmem_limit_bytes=16 << 20),
        cost_estimate=pl.CostEstimate(flops=2 * 10 ** 9, bytes_accessed=2 << 20, transcendentals=0),
    )(taps, taps, basis)

    residual, keep, give = pl.pallas_call(
        sky_kernel,
        out_shape=(
            jax.ShapeDtypeStruct((TR, TW), f32),
            jax.ShapeDtypeStruct((128, PS), f32),
            jax.ShapeDtypeStruct((128, PS), f32),
        ),
        in_specs=[SM, SM, SM] + [VM] * 6,
        out_specs=(VM, VM, VM),
        scratch_shapes=[
            pltpu.VMEM((32 * SROWS, 128), f32),
            pltpu.VMEM((5 * XROWS, 128), f32),
            pltpu.VMEM((256, PS), f32),
            pltpu.SMEM((SLOTS + GROUP,), jnp.int32),
        ] + [pltpu.VMEM((5 * CROWS, 128), f32)] * NCANV,
        compiler_params=pltpu.CompilerParams(vmem_limit_bytes=40 << 20),
        cost_estimate=pl.CostEstimate(flops=4 * 10 ** 9, bytes_accessed=4 << 20, transcendentals=0),
    )(spots, spots_up, spots_down, shaped, slot_params, obs, back, halo_up, halo_down)

    swap = [(i, i ^ 1) for i in range(16)]
    mine = keep + lax.ppermute(give, "epoch", swap)
    sent = jnp.broadcast_to(mine.reshape(n, 1, 8, PS), (n, 8, 8, PS)).reshape(128, 8, PS)
    groups = [[t * 16 + z * 2 + c for t in range(16) for z in range(8)] for c in range(2)]
    got = lax.all_to_all(sent, ("sky", "epoch"), split_axis=0, concat_axis=0, tiled=True, axis_index_groups=groups)
    part = pl.pallas_call(
        owner_kernel,
        out_shape=jax.ShapeDtypeStruct((128, PS), f32),
        in_specs=[SM, VM],
        out_specs=VM,
        scratch_shapes=[pltpu.VMEM((128, 128), f32)],
        compiler_params=pltpu.CompilerParams(vmem_limit_bytes=8 << 20),
    )(index, got)
    grad = part + lax.ppermute(part, "epoch", swap)
    return grad, residual[None]


def solution(mesh):
    in_specs = (
        P("sky", None),
        P(),
        P("epoch", None, None),
        P("sky", None, None),
        P("sky", None),
        P("sky", None, None),
        P("sky", None, None),
        P("epoch", "sky", None),
        P("epoch", "sky", None),
    )
    out_specs = (P("sky", None), P("epoch", "sky", None))
    return jax.shard_map(on_device, mesh=mesh, in_specs=in_specs, out_specs=out_specs, check_vma=False)
```

```python
import jax
import jax.numpy as jnp
from jax import lax
from jax.experimental import pallas as pl
from jax.experimental.pallas import tpu as pltpu
from jax.sharding import PartitionSpec as P

PS = 64
TAPS = 51
HALF = 25
TR = 256
TW = 512
CAP = 16
NSKY = 16
OWN = 256
SLOTS = 768
SROWS = 776
OFF = 64
CROWS = 448
XROWS = 320
PLANES = 8
PAIRS = 1
GROUP = 8
CHUNKS = 16
BLOCK = 64
DEAD = 128
HIGHEST = lax.Precision.HIGHEST
F32 = jnp.float32
BF16 = jnp.bfloat16


def dot(a, b, dims, precision=None):
    return lax.dot_general(a, b, (dims, ((), ())), precision=precision, preferred_element_type=F32)


def split3(x):
    high = x.astype(BF16)
    rest = x - high.astype(F32)
    mid = rest.astype(BF16)
    low = (rest - mid.astype(F32)).astype(BF16)
    return high, mid, low


def iota(shape, axis):
    return lax.broadcasted_iota(jnp.int32, shape, axis)


def send_kernel(index_s, count_s, params_ref, row_ref, col_ref, out_ref, hot):
    lane = iota((1, 128), 1)
    for t in range(NSKY):
        for k in range(CAP):
            hot[t * 16 + k:t * 16 + k + 1, :] = jnp.where(lane == index_s[t, k], 1.0, 0.0).astype(F32)
    rows = dot(hot[...].astype(BF16), params_ref[...], ((1,), (1,)))
    rows = jnp.concatenate([rows, rows], axis=1).astype(BF16)
    none = jnp.zeros((16, 128), BF16)
    owner, k_at = iota((NSKY, CAP), 0), iota((NSKY, CAP), 1)
    count = jnp.zeros((NSKY, CAP), jnp.int32)
    for o in range(NSKY):
        count = jnp.where(owner == o, count_s[0, o], count)
    row = jnp.where(k_at < count, row_ref[...], DEAD)
    col = col_ref[...]
    spots = jnp.concatenate([row, col >> 1, col & 1, jnp.zeros((NSKY, 80), jnp.int32)], axis=1)
    spots = spots.astype(F32).astype(BF16)
    for t in range(NSKY):
        mine = rows[t * 16:(t + 1) * 16]
        out_ref[t, 16:32, :] = mine
        if t + 1 < NSKY:
            out_ref[t + 1, 0:16, :] = mine
        if t > 0:
            out_ref[t - 1, 32:48, :] = mine
        out_ref[t, 48:64, :] = spots
    out_ref[0, 0:16, :] = none
    out_ref[NSKY - 1, 32:48, :] = none


def basis_kernel(taps_ref, basis_ref, out_ref, taps_pad, xs, ts):
    taps_pad[...] = jnp.zeros((8, 128), F32)
    taps = taps_ref[...]
    taps_pad[0:2, 0:TAPS] = taps / jnp.sum(taps, axis=1, keepdims=True)
    lane = iota((64, 128), 1)

    row_taps = jnp.broadcast_to(taps_pad[0:1, :], (32, 128))
    even = pltpu.roll(pltpu.roll(row_taps, 128 - HALF, 1), 0, 1, stride=2, stride_axis=0)
    odd = pltpu.roll(even, 1, 1)
    row_k = jnp.where(lane[:32] < 64, even, pltpu.roll(odd, 64, 1))
    parts = [x.astype(F32) for x in split3(row_k)] + [jnp.zeros((32, 128), F32)]
    row_parts = jnp.concatenate(parts, axis=0).T.astype(BF16)

    col_taps = jnp.broadcast_to(taps_pad[1:2, :], (64, 128))
    col_k = pltpu.roll(pltpu.roll(col_taps, 128 - HALF, 1), 0, 1, stride=1, stride_axis=0)
    left = jnp.where(lane < 64, col_k, 0.0)
    right = jnp.where(lane < 64, 0.0, pltpu.roll(col_k, 64, 1))
    none = jnp.zeros((64, 128), F32)
    col_k = jnp.concatenate([
        jnp.concatenate([left, none], axis=1), jnp.concatenate([right, none], axis=1),
        jnp.concatenate([none, left], axis=1), jnp.concatenate([none, right], axis=1)], axis=0)
    ch, cm, cl = split3(col_k)
    col_parts = jnp.concatenate([ch, cl, cm, ch, cm, ch], axis=0)

    for j in range(32):
        xs[j * 64:(j + 1) * 64, :] = basis_ref[:, j * 128:(j + 1) * 128].astype(F32)
    for g in range(8):
        images = [xs[pl.ds(g * 8 + i, 32, stride=64), :].astype(BF16) for i in range(8)]
        wide = jnp.concatenate(images, axis=1)
        made = dot(row_parts, jnp.concatenate([wide, wide, wide, wide], axis=0), ((1,), (0,)))
        for i in range(8):
            both = jnp.where(lane < 64, made[:64, i * 128:(i + 1) * 128], made[64:, i * 128:(i + 1) * 128])
            both = both + pltpu.roll(both, 64, 1)
            ts[pl.ds(g * 8 + i, 32, stride=64), :] = jnp.where(lane[:32] < 64, both[:32], both[32:])
    for m in range(4):
        x = jnp.concatenate([
            jnp.concatenate([ts[c * 128:c * 128 + 64, :], ts[c * 128 + 64:c * 128 + 128, :]], axis=1)
            for c in range(m * 4, m * 4 + 4)], axis=0)
        xh, xm, xl = split3(x)
        y = dot(jnp.concatenate([xl, xh, xm, xm, xh, xh], axis=1), col_parts, ((1,), (0,)))
        for part, v in enumerate(split3(y)):
            for i in range(4):
                out_ref[m * 4 + i, part * 64:(part + 1) * 64, :] = v[i * 64:(i + 1) * 64]


def sky_kernel(row_s, col_s, count_s, b_ref, got_ref, obs_ref, back_ref, halo_up_ref, halo_down_ref,
               res_ref, keep_ref, give_ref, ss, xs, xt, acc, near, packed, spots_v, spots_s, listed, sem, *canvases):
    tile = lax.axis_index("sky")
    core = lax.axis_index("epoch") % 2
    lane32 = iota((32, 128), 1)

    def spots_of(which, there):
        spots = got_ref[which, 48:64, :].astype(F32)
        row = spots.astype(jnp.int32)
        col = 2 * pltpu.roll(spots, 112, 1).astype(jnp.int32) + pltpu.roll(spots, 96, 1).astype(jnp.int32)
        return row, col

    row, col = spots_of(jnp.maximum(tile - 1, 0), None)
    spots_v[0:16, :] = jnp.where((row > 192) & (tile > 0), (row - TR + OFF) * 512 + col, -1)
    row, col = spots_of(jnp.minimum(tile + 1, NSKY - 1), None)
    spots_v[16:32, :] = jnp.where((row < 64) & (tile < NSKY - 1), (row + TR + OFF) * 512 + col, -1)
    copy = pltpu.make_async_copy(spots_v, spots_s, sem)
    copy.start()

    k_at = iota((CAP, 128), 0)
    mine = []
    for o in range(NSKY):
        mine.append(jnp.where(k_at < count_s[0, o], got_ref[o, 16:32, :].astype(F32), 0.0).astype(BF16))
        near[o * 32:o * 32 + 16, :] = got_ref[o, 0:16, :].astype(F32)
        near[o * 32 + 16:o * 32 + 32, :] = got_ref[o, 32:48, :].astype(F32)

    def three(x):
        return jnp.concatenate([x, x[:, :64]], axis=1)

    mine = three(jnp.concatenate(mine, axis=0))
    for j in range(32):
        ss[j * SROWS + SLOTS:(j + 1) * SROWS, :] = jnp.zeros((SROWS - SLOTS, 128), F32)
    copy.wait()

    span = PLANES * CROWS // CHUNKS

    def render(c, count):
        made = dot(mine, b_ref[c], ((1,), (0,)))
        made = made.astype(BF16).astype(F32)
        base = pl.multiple_of(c * (2 * SROWS), 8)
        ss[pl.ds(base, OWN), :] = made[:, :128]
        ss[pl.ds(base + SROWS, OWN), :] = made[:, 128:]
        for canvas in canvases:
            canvas[pl.ds(pl.multiple_of(c * span, 8), span), :] = jnp.zeros((span, 128), F32)
        for which in range(2):
            for k in range(CAP):
                entry = spots_s[which * 16 + c, k]
                listed[count] = entry
                packed[pl.ds(count, 1), :] = near[pl.ds(c * 32 + which * 16 + k, 1), :]
                count = count + jnp.where(entry >= 0, 1, 0)
        return count

    count = lax.fori_loop(0, CHUNKS, render, jnp.int32(0))

    def render_near(b, unused):
        base = pl.multiple_of(b * BLOCK, BLOCK)
        x = three(packed[pl.ds(base, BLOCK), :].astype(BF16))
        for c in range(CHUNKS):
            made = dot(x, b_ref[c], ((1,), (0,))).astype(BF16).astype(F32)
            ss[pl.ds(2 * c * SROWS + OWN + base, BLOCK), :] = made[:, :128]
            ss[pl.ds((2 * c + 1) * SROWS + OWN + base, BLOCK), :] = made[:, 128:]
        return unused

    lax.fori_loop(0, (count + BLOCK - 1) // BLOCK, render_near, 0)

    def put(i, slot, row, col):
        turn = col & 127
        start = (col >> 6) * CROWS + row
        turned = pltpu.roll(ss[pl.ds(slot, 32, stride=SROWS), :], turn, 1)
        inside = ((lane32 - turn) & 127) < 64
        canvases[2 * i][pl.ds(start, 32), :] += jnp.where(inside, turned, 0.0)
        canvases[2 * i + 1][pl.ds(start + 32, 32), :] += jnp.where(inside, 0.0, turned)

    def place(g, unused):
        for i in range(CAP):
            put(i % PAIRS, g * CAP + i, row_s[g, i] + OFF, col_s[g, i])
        return unused

    lax.fori_loop(0, NSKY, place, 0)

    def place_near(g, unused):
        for i in range(GROUP):
            at = g * GROUP + i
            real = at < count
            entry = jnp.where(real, listed[at], OFF * 512)
            put(i % PAIRS, jnp.where(real, OWN + at, SLOTS), entry >> 9, entry & 511)
        return unused

    lax.fori_loop(0, (count + GROUP - 1) // GROUP, place_near, 0)

    def pixels(observed, background, image):
        e = jnp.exp(-jnp.abs(image))
        soft = jnp.maximum(image, 0.0) + jnp.log1p(e)
        sig = jnp.where(image >= 0.0, 1.0, e) / (1.0 + e)
        return (observed / (background + soft) - 1.0) * sig

    def images(row, rows):
        left = iota((rows, 128), 1) < 64

        def planes(parity):
            out = []
            for h in range(PLANES):
                at = pl.ds(h * CROWS + OFF + row, rows)
                plane = canvases[parity][at, :]
                for i in range(1, PAIRS):
                    plane = plane + canvases[2 * i + parity][at, :]
                out.append(plane)
            return out

        upper, lower = planes(0), planes(1)
        out = []
        for q in range(4):
            before = jnp.zeros((rows, 128), F32) if q == 0 else upper[2 * q - 1]
            image = upper[2 * q] + jnp.where(left, before, upper[2 * q + 1])
            before = jnp.zeros((rows, 128), F32) if q == 0 else lower[2 * q - 1]
            out.append(image + pltpu.roll(lower[2 * q] + jnp.where(left, lower[2 * q + 1], before), 64, 1))
        return out

    def reach(row, rows, values):
        values = [v.astype(BF16).astype(F32) for v in values]
        turned = [pltpu.roll(v, 64, 1) for v in values]
        left = iota((rows, 128), 1) < 64
        for q in range(4):
            after = min(q + 1, 3)
            even, odd = pl.ds(2 * q * XROWS + row, rows), pl.ds((2 * q + 1) * XROWS + row, rows)
            xs[even, :] = values[q]
            xs[odd, :] = jnp.where(left, values[after], values[q])
            xt[even, :] = turned[q]
            xt[odd, :] = jnp.where(left, turned[q], turned[after])

    def edge(halo, row, real):
        values = []
        for q, image in enumerate(images(row, 32)):
            lanes = slice(q * 128, (q + 1) * 128)
            values.append(jnp.where(real, pixels(halo[:32, lanes], halo[32:, lanes], image), 0.0))
        reach(row, 32, values)

    edge(halo_up_ref, 0, tile > 0)
    edge(halo_down_ref, 288, tile < NSKY - 1)

    def block(i, unused):
        base = pl.multiple_of(i * 32, 32)
        values = []
        for q, image in enumerate(images(32 + base, 32)):
            lanes = slice(q * 128, (q + 1) * 128)
            r = pixels(obs_ref[pl.ds(base, 32), lanes], back_ref[pl.ds(base, 32), lanes], image)
            res_ref[pl.ds(base, 32), lanes] = r
            values.append(r)
        reach(32 + base, 32, values)
        return unused

    lax.fori_loop(0, 8, block, 0)

    def window(g, unused):
        for i in range(CAP):
            row, col = row_s[g, i], col_s[g, i]
            turn = col & 127
            start = (col >> 6) * XROWS + row
            inside = ((lane32 - turn) & 127) < 64
            seen = jnp.where(inside, xs[pl.ds(start, 32), :], xt[pl.ds(start + 32, 32), :])
            ss[pl.ds(g * CAP + i, 32, stride=SROWS), :] = pltpu.roll(seen, (128 - turn) & 127, 1)
        return unused

    lax.fori_loop(0, NSKY, window, 0)

    total = jnp.zeros((OWN, 192), F32)
    for c in range(CHUNKS):
        base = 2 * c * SROWS
        w = jnp.concatenate([ss[base:base + OWN, :], ss[base + SROWS:base + SROWS + OWN, :]], axis=1).astype(BF16)
        total = total + dot(w, b_ref[c], ((1,), (1,)))
    grad = total[:, 128:192] + total[:, 64:128] + total[:, :64]
    grad = jnp.concatenate([grad, grad], axis=1)
    for o in range(NSKY):
        acc[o * 16:(o + 1) * 16, :] = jnp.where(k_at < count_s[0, o], grad[o * 16:(o + 1) * 16], 0.0)
    left = iota((4, 128), 1) < 64
    for o in range(NSKY):
        for ref, at in ((keep_ref, o * 16 + core * 8), (give_ref, o * 16 + 8 - core * 8)):
            ref[o] = jnp.where(left, acc[pl.ds(at, 4), :], acc[pl.ds(at + 4, 4), :])


def owner_kernel(index_s, got_ref, out_ref, first, second, sums):
    core = lax.axis_index("epoch") % 2
    lane = iota((1, 128), 1)
    for t in range(NSKY):
        for r in range(4):
            for hot, k in ((first, r), (second, r + 4)):
                hot[t * 4 + r:t * 4 + r + 1, :] = jnp.where(lane == index_s[t, core * 8 + k], 1.0, 0.0).astype(F32)
    for t in range(NSKY):
        s = got_ref[t * 8]
        for z in range(1, 8):
            s = s + got_ref[t * 8 + z]
        sums[t * 4:(t + 1) * 4, :] = s
    x = sums[...]
    out = dot(x, first[...], ((0,), (0,)), HIGHEST)[:64] + dot(x, second[...], ((0,), (0,)), HIGHEST)[64:]
    out_ref[...] = out


SM = pl.BlockSpec(memory_space=pltpu.SMEM)
VM = pl.BlockSpec(memory_space=pltpu.VMEM)


def call_send(index, count, params_t, row, col):
    return pl.pallas_call(
        send_kernel,
        out_shape=jax.ShapeDtypeStruct((NSKY, 64, 128), BF16),
        in_specs=[SM, SM, VM, VM, VM],
        out_specs=VM,
        scratch_shapes=[pltpu.VMEM((256, 128), F32)],
        compiler_params=pltpu.CompilerParams(vmem_limit_bytes=8 << 20),
    )(index, count, params_t, row, col)


def call_basis(taps, basis):
    return pl.pallas_call(
        basis_kernel,
        out_shape=jax.ShapeDtypeStruct((CHUNKS, 192, 256), BF16),
        in_specs=[VM, VM],
        out_specs=VM,
        scratch_shapes=[
            pltpu.VMEM((8, 128), F32),
            pltpu.VMEM((33 * 64, 128), F32),
            pltpu.VMEM((33 * 64, 128), F32),
        ],
        compiler_params=pltpu.CompilerParams(vmem_limit_bytes=16 << 20),
        cost_estimate=pl.CostEstimate(flops=2 * 10 ** 9, bytes_accessed=2 << 20, transcendentals=0),
    )(taps, basis)


def call_sky(row, col, count, shaped, got, obs, back, halo_up, halo_down):
    return pl.pallas_call(
        sky_kernel,
        out_shape=(
            jax.ShapeDtypeStruct((TR, TW), F32),
            jax.ShapeDtypeStruct((NSKY, 4, 128), F32),
            jax.ShapeDtypeStruct((NSKY, 4, 128), F32),
        ),
        in_specs=[SM, SM, SM] + [VM] * 6,
        out_specs=(VM, VM, VM),
        scratch_shapes=[
            pltpu.VMEM((33 * SROWS, 128), F32),
            pltpu.VMEM((PLANES * XROWS, 128), F32),
            pltpu.VMEM((PLANES * XROWS, 128), F32),
            pltpu.VMEM((OWN, 128), F32),
            pltpu.VMEM((512, 128), F32),
            pltpu.VMEM((520, 128), F32),
            pltpu.VMEM((32, 128), jnp.int32),
            pltpu.SMEM((32, 128), jnp.int32),
            pltpu.SMEM((520,), jnp.int32),
            pltpu.SemaphoreType.DMA,
        ] + [pltpu.VMEM((PLANES * CROWS, 128), F32)] * (2 * PAIRS),
        compiler_params=pltpu.CompilerParams(vmem_limit_bytes=32 << 20),
        cost_estimate=pl.CostEstimate(flops=4 * 10 ** 9, bytes_accessed=4 << 20, transcendentals=0),
    )(row, col, count, shaped, got, obs, back, halo_up, halo_down)


def call_owner(index, got):
    return pl.pallas_call(
        owner_kernel,
        out_shape=jax.ShapeDtypeStruct((PS, 128), F32),
        in_specs=[SM, VM],
        out_specs=VM,
        scratch_shapes=[pltpu.VMEM((64, 128), F32)] * 3,
        compiler_params=pltpu.CompilerParams(vmem_limit_bytes=8 << 20),
    )(index, got)


def on_device(params, basis, psf_taps, send_index, tile_count, stamp_row, stamp_col, observed, background):
    n = NSKY
    index = send_index[0]
    row, col = stamp_row[0], stamp_col[0]
    obs, back = observed[0], background[0]
    sent = call_send(index, tile_count, params.T, row, col)
    got = lax.all_to_all(sent, "sky", split_axis=0, concat_axis=0, tiled=True)
    to_next = [(i, i + 1) for i in range(n - 1)]
    to_prev = [(i + 1, i) for i in range(n - 1)]
    halo_up = lax.ppermute(jnp.concatenate([obs[TR - 32:], back[TR - 32:]], axis=0), "sky", to_next)
    halo_down = lax.ppermute(jnp.concatenate([obs[:32], back[:32]], axis=0), "sky", to_prev)
    shaped = call_basis(psf_taps[0], basis)
    residual, keep, give = call_sky(row, col, tile_count, shaped, got, obs, back, halo_up, halo_down)
    swap = [(i, i ^ 1) for i in range(16)]
    mine = keep + lax.ppermute(give, "epoch", swap)
    spread = jnp.broadcast_to(mine[:, None], (n, 8, 4, 128)).reshape(128, 4, 128)
    groups = [[t * 16 + z * 2 + c for t in range(16) for z in range(8)] for c in range(2)]
    back_home = lax.all_to_all(
        spread, ("sky", "epoch"), split_axis=0, concat_axis=0, tiled=True, axis_index_groups=groups
    )
    part = call_owner(index, back_home)
    grad = part + lax.ppermute(part, "epoch", swap)
    return grad.T, residual[None]


def solution(mesh):
    in_specs = (
        P("sky", None),
        P(),
        P("epoch", None, None),
        P("sky", None, None),
        P("sky", None),
        P("sky", None, None),
        P("sky", None, None),
        P("epoch", "sky", None),
        P("epoch", "sky", None),
    )
    out_specs = (P("sky", None), P("epoch", "sky", None))
    return jax.shard_map(on_device, mesh=mesh, in_specs=in_specs, out_specs=out_specs, check_vma=False)
```

```python
import jax
import jax.numpy as jnp
from jax import lax
from jax.experimental import pallas as pl
from jax.experimental.pallas import tpu as pltpu
from jax.sharding import PartitionSpec as P

PS = 64
TAPS = 51
HALF = 25
TR = 256
TW = 512
CAP = 16
NSKY = 16
OWN = 256
SLOTS = 768
SROWS = 776
OFF = 64
CROWS = 448
XROWS = 320
PLANES = 8
PAIRS = 2
GROUP = 16
CHUNKS = 16
BLOCK = 128
DEAD = 128
HIGHEST = lax.Precision.HIGHEST
F32 = jnp.float32
BF16 = jnp.bfloat16


def dot(a, b, dims, precision=None):
    return lax.dot_general(a, b, (dims, ((), ())), precision=precision, preferred_element_type=F32)


def split3(x):
    high = x.astype(BF16)
    rest = x - high.astype(F32)
    mid = rest.astype(BF16)
    low = (rest - mid.astype(F32)).astype(BF16)
    return high, mid, low


def iota(shape, axis):
    return lax.broadcasted_iota(jnp.int32, shape, axis)


def send_kernel(index_s, count_s, params_ref, row_ref, col_ref, out_ref, hot):
    lane = iota((1, 128), 1)
    for t in range(NSKY):
        for k in range(CAP):
            hot[t * 16 + k:t * 16 + k + 1, :] = jnp.where(lane == index_s[t, k], 1.0, 0.0).astype(F32)
    rows = dot(hot[...].astype(BF16), params_ref[...], ((1,), (1,)))
    rows = jnp.concatenate([rows, rows], axis=1).astype(BF16)
    none = jnp.zeros((16, 128), BF16)
    owner, k_at = iota((NSKY, CAP), 0), iota((NSKY, CAP), 1)
    count = jnp.zeros((NSKY, CAP), jnp.int32)
    for o in range(NSKY):
        count = jnp.where(owner == o, count_s[0, o], count)
    row = jnp.where(k_at < count, row_ref[...], DEAD)
    col = col_ref[...]
    spots = jnp.concatenate([row, col >> 1, col & 1, jnp.zeros((NSKY, 80), jnp.int32)], axis=1)
    spots = spots.astype(F32).astype(BF16)
    for t in range(NSKY):
        mine = rows[t * 16:(t + 1) * 16]
        out_ref[t, 16:32, :] = mine
        if t + 1 < NSKY:
            out_ref[t + 1, 0:16, :] = mine
        if t > 0:
            out_ref[t - 1, 32:48, :] = mine
        out_ref[t, 48:64, :] = spots
    out_ref[0, 0:16, :] = none
    out_ref[NSKY - 1, 32:48, :] = none


def basis_kernel(taps_ref, basis_ref, out_hbm, taps_pad, xs, ts, out_ref, sems):
    taps_pad[...] = jnp.zeros((8, 128), F32)
    taps = taps_ref[...]
    taps_pad[0:2, 0:TAPS] = taps / jnp.sum(taps, axis=1, keepdims=True)
    lane = iota((64, 128), 1)

    row_taps = jnp.broadcast_to(taps_pad[0:1, :], (32, 128))
    even = pltpu.roll(pltpu.roll(row_taps, 128 - HALF, 1), 0, 1, stride=2, stride_axis=0)
    odd = pltpu.roll(even, 1, 1)
    row_k = jnp.where(lane[:32] < 64, even, pltpu.roll(odd, 64, 1))
    parts = [x.astype(F32) for x in split3(row_k)] + [jnp.zeros((32, 128), F32)]
    row_parts = jnp.concatenate(parts, axis=0).T.astype(BF16)

    col_taps = jnp.broadcast_to(taps_pad[1:2, :], (64, 128))
    col_k = pltpu.roll(pltpu.roll(col_taps, 128 - HALF, 1), 0, 1, stride=1, stride_axis=0)
    left = jnp.where(lane < 64, col_k, 0.0)
    right = jnp.where(lane < 64, 0.0, pltpu.roll(col_k, 64, 1))
    none = jnp.zeros((64, 128), F32)
    col_k = jnp.concatenate([
        jnp.concatenate([left, none], axis=1), jnp.concatenate([right, none], axis=1),
        jnp.concatenate([none, left], axis=1), jnp.concatenate([none, right], axis=1)], axis=0)
    ch, cm, cl = split3(col_k)
    col_parts = jnp.concatenate([ch, cl, cm, ch, cm, ch], axis=0)

    for j in range(32):
        xs[j * 64:(j + 1) * 64, :] = basis_ref[:, j * 128:(j + 1) * 128].astype(F32)
    for g in range(8):
        images = [xs[pl.ds(g * 8 + i, 32, stride=64), :].astype(BF16) for i in range(8)]
        wide = jnp.concatenate(images, axis=1)
        made = dot(row_parts, jnp.concatenate([wide, wide, wide, wide], axis=0), ((1,), (0,)))
        for i in range(8):
            both = jnp.where(lane < 64, made[:64, i * 128:(i + 1) * 128], made[64:, i * 128:(i + 1) * 128])
            both = both + pltpu.roll(both, 64, 1)
            ts[pl.ds(g * 8 + i, 32, stride=64), :] = jnp.where(lane[:32] < 64, both[:32], both[32:])
    copies = []
    for m in range(4):
        x = jnp.concatenate([
            jnp.concatenate([ts[c * 128:c * 128 + 64, :], ts[c * 128 + 64:c * 128 + 128, :]], axis=1)
            for c in range(m * 4, m * 4 + 4)], axis=0)
        xh, xm, xl = split3(x)
        y = dot(jnp.concatenate([xl, xh, xm, xm, xh, xh], axis=1), col_parts, ((1,), (0,)))
        for part, v in enumerate(split3(y)):
            for i in range(4):
                out_ref[m * 4 + i, part * 64:(part + 1) * 64, :] = v[i * 64:(i + 1) * 64]
        copies.append(pltpu.make_async_copy(out_ref.at[pl.ds(m * 4, 4)], out_hbm.at[pl.ds(m * 4, 4)], sems.at[m]))
        copies[-1].start()
    for copy in copies:
        copy.wait()


def sky_kernel(row_s, col_s, count_s, b_hbm, got_ref, obs_hbm, back_hbm, halo_up_ref, halo_down_ref,
               res_hbm, keep_ref, give_ref, b_ref, obs_ref, back_ref, res_ref, sems, ss, xs, xt, acc, near, packed, spots_v, spots_s, listed, sem, *canvases):
    tile = lax.axis_index("sky")
    core = lax.axis_index("epoch") % 2
    lane32 = iota((32, 128), 1)
    b_copy = pltpu.make_async_copy(b_hbm, b_ref, sems.at[0])
    b_copy.start()
    late = [pltpu.make_async_copy(obs_hbm, obs_ref, sems.at[1]), pltpu.make_async_copy(back_hbm, back_ref, sems.at[2])]
    for each in late:
        each.start()

    def spots_of(which, there):
        spots = got_ref[which, 48:64, :].astype(F32)
        row = spots.astype(jnp.int32)
        col = 2 * pltpu.roll(spots, 112, 1).astype(jnp.int32) + pltpu.roll(spots, 96, 1).astype(jnp.int32)
        return row, col

    row, col = spots_of(jnp.maximum(tile - 1, 0), None)
    spots_v[0:16, :] = jnp.where((row > 192) & (tile > 0), (row - TR + OFF) * 512 + col, -1)
    row, col = spots_of(jnp.minimum(tile + 1, NSKY - 1), None)
    spots_v[16:32, :] = jnp.where((row < 64) & (tile < NSKY - 1), (row + TR + OFF) * 512 + col, -1)
    copy = pltpu.make_async_copy(spots_v, spots_s, sem)
    copy.start()

    k_at = iota((CAP, 128), 0)
    mine = []
    for o in range(NSKY):
        mine.append(jnp.where(k_at < count_s[0, o], got_ref[o, 16:32, :].astype(F32), 0.0).astype(BF16))
        near[o * 32:o * 32 + 16, :] = got_ref[o, 0:16, :].astype(F32)
        near[o * 32 + 16:o * 32 + 32, :] = got_ref[o, 32:48, :].astype(F32)

    def three(x):
        return jnp.concatenate([x, x[:, :64]], axis=1)

    mine = three(jnp.concatenate(mine, axis=0))
    for j in range(32):
        ss[j * SROWS + SLOTS:(j + 1) * SROWS, :] = jnp.zeros((SROWS - SLOTS, 128), F32)
    copy.wait()
    b_copy.wait()

    span = PLANES * CROWS // CHUNKS

    def render(c, count):
        made = dot(mine, b_ref[c], ((1,), (0,)))
        made = made.astype(BF16).astype(F32)
        base = pl.multiple_of(c * (2 * SROWS), 8)
        ss[pl.ds(base, OWN), :] = made[:, :128]
        ss[pl.ds(base + SROWS, OWN), :] = made[:, 128:]
        for canvas in canvases:
            canvas[pl.ds(pl.multiple_of(c * span, 8), span), :] = jnp.zeros((span, 128), F32)
        for which in range(2):
            for k in range(CAP):
                entry = spots_s[which * 16 + c, k]
                listed[count] = entry
                packed[pl.ds(count, 1), :] = near[pl.ds(c * 32 + which * 16 + k, 1), :]
                count = count + jnp.where(entry >= 0, 1, 0)
        return count

    count = lax.fori_loop(0, CHUNKS, render, jnp.int32(0), unroll=4)

    def render_near(b, unused):
        base = pl.multiple_of(b * BLOCK, BLOCK)
        x = three(packed[pl.ds(base, BLOCK), :].astype(BF16))
        for c in range(CHUNKS):
            made = dot(x, b_ref[c], ((1,), (0,))).astype(BF16).astype(F32)
            ss[pl.ds(2 * c * SROWS + OWN + base, BLOCK), :] = made[:, :128]
            ss[pl.ds((2 * c + 1) * SROWS + OWN + base, BLOCK), :] = made[:, 128:]
        return unused

    lax.fori_loop(0, (count + BLOCK - 1) // BLOCK, render_near, 0)

    def put(i, slot, row, col):
        turn = col & 127
        start = (col >> 6) * CROWS + row
        turned = pltpu.roll(ss[pl.ds(slot, 32, stride=SROWS), :], turn, 1)
        inside = ((lane32 - turn) & 127) < 64
        canvases[2 * i][pl.ds(start, 32), :] += jnp.where(inside, turned, 0.0)
        canvases[2 * i + 1][pl.ds(start + 32, 32), :] += jnp.where(inside, 0.0, turned)

    def place(g, unused):
        for i in range(CAP):
            put(i % PAIRS, g * CAP + i, row_s[g, i] + OFF, col_s[g, i])
        return unused

    lax.fori_loop(0, NSKY, place, 0, unroll=4)

    def place_near(g, unused):
        for i in range(GROUP):
            at = g * GROUP + i
            real = at < count
            entry = jnp.where(real, listed[at], OFF * 512)
            put(i % PAIRS, jnp.where(real, OWN + at, SLOTS), entry >> 9, entry & 511)
        return unused

    lax.fori_loop(0, (count + GROUP - 1) // GROUP, place_near, 0)

    for each in late:
        each.wait()

    def pixels(observed, background, image):
        e = jnp.exp(-jnp.abs(image))
        soft = jnp.maximum(image, 0.0) + jnp.log1p(e)
        sig = jnp.where(image >= 0.0, 1.0, e) / (1.0 + e)
        return (observed / (background + soft) - 1.0) * sig

    def images(row, rows):
        left = iota((rows, 128), 1) < 64

        def planes(parity):
            out = []
            for h in range(PLANES):
                at = pl.ds(h * CROWS + OFF + row, rows)
                plane = canvases[parity][at, :]
                for i in range(1, PAIRS):
                    plane = plane + canvases[2 * i + parity][at, :]
                out.append(plane)
            return out

        upper, lower = planes(0), planes(1)
        out = []
        for q in range(4):
            before = jnp.zeros((rows, 128), F32) if q == 0 else upper[2 * q - 1]
            image = upper[2 * q] + jnp.where(left, before, upper[2 * q + 1])
            before = jnp.zeros((rows, 128), F32) if q == 0 else lower[2 * q - 1]
            out.append(image + pltpu.roll(lower[2 * q] + jnp.where(left, lower[2 * q + 1], before), 64, 1))
        return out

    def reach(row, rows, values):
        values = [v.astype(BF16).astype(F32) for v in values]
        turned = [pltpu.roll(v, 64, 1) for v in values]
        left = iota((rows, 128), 1) < 64
        for q in range(4):
            after = min(q + 1, 3)
            even, odd = pl.ds(2 * q * XROWS + row, rows), pl.ds((2 * q + 1) * XROWS + row, rows)
            xs[even, :] = values[q]
            xs[odd, :] = jnp.where(left, values[after], values[q])
            xt[even, :] = turned[q]
            xt[odd, :] = jnp.where(left, turned[q], turned[after])

    def edge(halo, row, real):
        values = []
        for q, image in enumerate(images(row, 32)):
            lanes = slice(q * 128, (q + 1) * 128)
            values.append(jnp.where(real, pixels(halo[:32, lanes], halo[32:, lanes], image), 0.0))
        reach(row, 32, values)

    edge(halo_up_ref, 0, tile > 0)
    edge(halo_down_ref, 288, tile < NSKY - 1)

    def block(i, unused):
        base = pl.multiple_of(i * 32, 32)
        values = []
        for q, image in enumerate(images(32 + base, 32)):
            lanes = slice(q * 128, (q + 1) * 128)
            r = pixels(obs_ref[pl.ds(base, 32), lanes], back_ref[pl.ds(base, 32), lanes], image)
            res_ref[pl.ds(base, 32), lanes] = r
            values.append(r)
        reach(32 + base, 32, values)
        return unused

    lax.fori_loop(0, 8, block, 0, unroll=8)
    res_copy = pltpu.make_async_copy(res_ref, res_hbm, sems.at[3])
    res_copy.start()

    def window(g, unused):
        for i in range(CAP):
            row, col = row_s[g, i], col_s[g, i]
            turn = col & 127
            start = (col >> 6) * XROWS + row
            inside = ((lane32 - turn) & 127) < 64
            seen = jnp.where(inside, xs[pl.ds(start, 32), :], xt[pl.ds(start + 32, 32), :])
            ss[pl.ds(g * CAP + i, 32, stride=SROWS), :] = pltpu.roll(seen, (128 - turn) & 127, 1)
        return unused

    lax.fori_loop(0, NSKY, window, 0, unroll=4)

    total = jnp.zeros((OWN, 192), F32)
    for c in range(CHUNKS):
        base = 2 * c * SROWS
        w = jnp.concatenate([ss[base:base + OWN, :], ss[base + SROWS:base + SROWS + OWN, :]], axis=1).astype(BF16)
        total = total + dot(w, b_ref[c], ((1,), (1,)))
    grad = total[:, 128:192] + total[:, 64:128] + total[:, :64]
    grad = jnp.concatenate([grad, grad], axis=1)
    for o in range(NSKY):
        acc[o * 16:(o + 1) * 16, :] = jnp.where(k_at < count_s[0, o], grad[o * 16:(o + 1) * 16], 0.0)
    left = iota((4, 128), 1) < 64
    for o in range(NSKY):
        for ref, at in ((keep_ref, o * 16 + core * 8), (give_ref, o * 16 + 8 - core * 8)):
            ref[o] = jnp.where(left, acc[pl.ds(at, 4), :], acc[pl.ds(at + 4, 4), :])
    res_copy.wait()


def owner_kernel(index_s, got_ref, out_ref, first, second, sums):
    core = lax.axis_index("epoch") % 2
    lane = iota((1, 128), 1)
    for t in range(NSKY):
        for r in range(4):
            for hot, k in ((first, r), (second, r + 4)):
                hot[t * 4 + r:t * 4 + r + 1, :] = jnp.where(lane == index_s[t, core * 8 + k], 1.0, 0.0).astype(F32)
    for t in range(NSKY):
        s = got_ref[t * 8]
        for z in range(1, 8):
            s = s + got_ref[t * 8 + z]
        sums[t * 4:(t + 1) * 4, :] = s
    x = sums[...]
    out = dot(x, first[...], ((0,), (0,)), HIGHEST)[:64] + dot(x, second[...], ((0,), (0,)), HIGHEST)[64:]
    out_ref[...] = out


ROOMY = 62_100_000
SM = pl.BlockSpec(memory_space=pltpu.SMEM)
HB = pl.BlockSpec(memory_space=pltpu.HBM)
VM = pl.BlockSpec(memory_space=pltpu.VMEM)


def call_send(index, count, params_t, row, col):
    return pl.pallas_call(
        send_kernel,
        out_shape=jax.ShapeDtypeStruct((NSKY, 64, 128), BF16),
        in_specs=[SM, SM, VM, VM, VM],
        out_specs=VM,
        scratch_shapes=[pltpu.VMEM((256, 128), F32)],
        compiler_params=pltpu.CompilerParams(vmem_limit_bytes=60 << 20),
        cost_estimate=pl.CostEstimate(flops=8 * 10 ** 9, bytes_accessed=16 << 20, transcendentals=0),
    )(index, count, params_t, row, col)


def call_basis(taps, basis):
    return pl.pallas_call(
        basis_kernel,
        out_shape=jax.ShapeDtypeStruct((CHUNKS, 192, 256), BF16),
        in_specs=[VM, VM],
        out_specs=HB,
        scratch_shapes=[
            pltpu.VMEM((8, 128), F32),
            pltpu.VMEM((33 * 64, 128), F32),
            pltpu.VMEM((33 * 64, 128), F32),
            pltpu.VMEM((CHUNKS, 192, 256), BF16),
            pltpu.SemaphoreType.DMA((4,)),
        ],
        compiler_params=pltpu.CompilerParams(vmem_limit_bytes=ROOMY),
        cost_estimate=pl.CostEstimate(flops=10 ** 5, bytes_accessed=1 << 10, transcendentals=0),
    )(taps, basis)


def call_sky(row, col, count, shaped, got, obs, back, halo_up, halo_down):
    return pl.pallas_call(
        sky_kernel,
        out_shape=(
            jax.ShapeDtypeStruct((TR, TW), F32),
            jax.ShapeDtypeStruct((NSKY, 4, 128), F32),
            jax.ShapeDtypeStruct((NSKY, 4, 128), F32),
        ),
        in_specs=[SM, SM, SM, HB, VM, HB, HB, VM, VM],
        out_specs=(HB, VM, VM),
        scratch_shapes=[
            pltpu.VMEM((CHUNKS, 192, 256), BF16),
            pltpu.VMEM((TR, TW), F32),
            pltpu.VMEM((TR, TW), F32),
            pltpu.VMEM((TR, TW), F32),
            pltpu.SemaphoreType.DMA((4,)),
            pltpu.VMEM((33 * SROWS, 128), F32),
            pltpu.VMEM((PLANES * XROWS, 128), F32),
            pltpu.VMEM((PLANES * XROWS, 128), F32),
            pltpu.VMEM((OWN, 128), F32),
            pltpu.VMEM((512, 128), F32),
            pltpu.VMEM((520, 128), F32),
            pltpu.VMEM((32, 128), jnp.int32),
            pltpu.SMEM((32, 128), jnp.int32),
            pltpu.SMEM((520,), jnp.int32),
            pltpu.SemaphoreType.DMA,
        ] + [pltpu.VMEM((PLANES * CROWS, 128), F32)] * (2 * PAIRS),
        compiler_params=pltpu.CompilerParams(vmem_limit_bytes=54_000_000),
        cost_estimate=pl.CostEstimate(flops=4 * 10 ** 9, bytes_accessed=4 << 20, transcendentals=0),
    )(row, col, count, shaped, got, obs, back, halo_up, halo_down)


def call_owner(index, got):
    return pl.pallas_call(
        owner_kernel,
        out_shape=jax.ShapeDtypeStruct((PS, 128), F32),
        in_specs=[SM, VM],
        out_specs=VM,
        scratch_shapes=[pltpu.VMEM((64, 128), F32)] * 3,
        compiler_params=pltpu.CompilerParams(vmem_limit_bytes=8 << 20),
    )(index, got)


def on_device(params, basis, psf_taps, send_index, tile_count, stamp_row, stamp_col, observed, background):
    n = NSKY
    index = send_index[0]
    row, col = stamp_row[0], stamp_col[0]
    obs, back = observed[0], background[0]
    low = jnp.concatenate([obs[TR - 32:], back[TR - 32:]], axis=0)
    high = jnp.concatenate([obs[:32], back[:32]], axis=0)
    sent = call_send(index, tile_count, params.T, row, col)
    got = lax.all_to_all(sent, "sky", split_axis=0, concat_axis=0, tiled=True)
    to_next = [(i, i + 1) for i in range(n - 1)]
    to_prev = [(i + 1, i) for i in range(n - 1)]
    halo_up = lax.ppermute(low, "sky", to_next)
    halo_down = lax.ppermute(high, "sky", to_prev)
    shaped = call_basis(psf_taps[0], basis)
    residual, keep, give = call_sky(row, col, tile_count, shaped, got, obs, back, halo_up, halo_down)
    swap = [(i, i ^ 1) for i in range(16)]
    mine = keep + lax.ppermute(give, "epoch", swap)
    spread = jnp.broadcast_to(mine[:, None], (n, 8, 4, 128)).reshape(128, 4, 128)
    groups = [[t * 16 + z * 2 + c for t in range(16) for z in range(8)] for c in range(2)]
    back_home = lax.all_to_all(
        spread, ("sky", "epoch"), split_axis=0, concat_axis=0, tiled=True, axis_index_groups=groups
    )
    part = call_owner(index, back_home)
    grad = part + lax.ppermute(part, "epoch", swap)
    return grad.T, residual[None]


def solution(mesh):
    in_specs = (
        P("sky", None),
        P(),
        P("epoch", None, None),
        P("sky", None, None),
        P("sky", None),
        P("sky", None, None),
        P("sky", None, None),
        P("epoch", "sky", None),
        P("epoch", "sky", None),
    )
    out_specs = (P("sky", None), P("epoch", "sky", None))
    return jax.shard_map(on_device, mesh=mesh, in_specs=in_specs, out_specs=out_specs, check_vma=False)
```

```python
import jax
import jax.numpy as jnp
from jax import lax
from jax.experimental import pallas as pl
from jax.experimental.pallas import tpu as pltpu
from jax.sharding import PartitionSpec as P

PS = 64
TAPS = 51
HALF = 25
TR = 256
TW = 512
CAP = 16
NSKY = 16
OWN = 256
SLOTS = 768
SROWS = 776
OFF = 64
CROWS = 448
XROWS = 320
PLANES = 8
PAIRS = 2
GROUP = 16
CHUNKS = 16
BLOCK = 128
STEP = 72
DEAD = 128
HIGHEST = lax.Precision.HIGHEST
F32 = jnp.float32
BF16 = jnp.bfloat16


def dot(a, b, dims, precision=None):
    return lax.dot_general(a, b, (dims, ((), ())), precision=precision, preferred_element_type=F32)


def split3(x):
    high = x.astype(BF16)
    rest = x - high.astype(F32)
    mid = rest.astype(BF16)
    low = (rest - mid.astype(F32)).astype(BF16)
    return high, mid, low


def iota(shape, axis):
    return lax.broadcasted_iota(jnp.int32, shape, axis)


def send_kernel(index_s, count_s, params_ref, row_ref, col_ref, obs_hbm, back_hbm, out_ref, first_ref, second_ref, hot, sems):
    even = lax.axis_index("sky") % 2 == 0
    copies = []
    for to, at in ((first_ref, jnp.where(even, TR - 32, 0)), (second_ref, jnp.where(even, 0, TR - 32))):
        for i, image in enumerate((obs_hbm, back_hbm)):
            rows = pl.ds(pl.multiple_of(at, 32), 32)
            copies.append(pltpu.make_async_copy(image.at[rows, :], to.at[pl.ds(32 * i, 32), :], sems.at[len(copies)]))
            copies[-1].start()
    lane = iota((1, 128), 1)
    for t in range(NSKY):
        for k in range(CAP):
            hot[t * 16 + k:t * 16 + k + 1, :] = jnp.where(lane == index_s[t, k], 1.0, 0.0).astype(F32)
    rows = dot(hot[...].astype(BF16), params_ref[...], ((1,), (1,)))
    rows = jnp.concatenate([rows, rows], axis=1).astype(BF16)
    none = jnp.zeros((16, 128), BF16)
    owner, k_at = iota((NSKY, CAP), 0), iota((NSKY, CAP), 1)
    count = jnp.zeros((NSKY, CAP), jnp.int32)
    for o in range(NSKY):
        count = jnp.where(owner == o, count_s[0, o], count)
    row = jnp.where(k_at < count, row_ref[...], DEAD)
    col = col_ref[...]
    spots = jnp.concatenate([row, col >> 1, col & 1, jnp.zeros((NSKY, 80), jnp.int32)], axis=1)
    spots = spots.astype(F32).astype(BF16)
    for t in range(NSKY):
        mine = rows[t * 16:(t + 1) * 16]
        out_ref[t, 16:32, :] = mine
        if t + 1 < NSKY:
            out_ref[t + 1, 0:16, :] = mine
        if t > 0:
            out_ref[t - 1, 32:48, :] = mine
        out_ref[t, 48:64, :] = spots
    out_ref[0, 0:16, :] = none
    out_ref[NSKY - 1, 32:48, :] = none
    for copy in copies:
        copy.wait()


def convolve(taps_ref, basis_ref, out_ref, taps_pad, xs, ts, beside):
    taps_pad[...] = jnp.zeros((8, 128), F32)
    taps = taps_ref[...]
    taps_pad[0:2, 0:TAPS] = taps / jnp.sum(taps, axis=1, keepdims=True)
    lane = iota((64, 128), 1)

    row_taps = jnp.broadcast_to(taps_pad[0:1, :], (32, 128))
    even = pltpu.roll(pltpu.roll(row_taps, 128 - HALF, 1), 0, 1, stride=2, stride_axis=0)
    odd = pltpu.roll(even, 1, 1)
    row_k = jnp.where(lane[:32] < 64, even, pltpu.roll(odd, 64, 1))
    rh, rm, rl = [x.astype(F32) for x in split3(row_k)]
    none = jnp.zeros((64, 128), F32)
    row_parts = jnp.concatenate([rl, rm, rh, rm, rh, rh, none], axis=0).T.astype(BF16)[:, :192]

    col_taps = jnp.broadcast_to(taps_pad[1:2, :], (64, 128))
    col_k = pltpu.roll(pltpu.roll(col_taps, 128 - HALF, 1), 0, 1, stride=1, stride_axis=0)
    col_k = jnp.concatenate([jnp.where(lane < 64, col_k, 0.0), jnp.where(lane < 64, 0.0, pltpu.roll(col_k, 64, 1))], axis=0)
    ch, cm, cl = split3(col_k)
    col_parts = jnp.concatenate([
        jnp.concatenate([ch, cm], axis=1), jnp.concatenate([cl, jnp.zeros((128, 128), BF16)], axis=1)], axis=0)

    for m in range(4):
        x = jnp.concatenate([basis_ref[:, j * 128:(j + 1) * 128] for j in range(m * 8, m * 8 + 8)], axis=0)
        made = dot(jnp.concatenate([x, x], axis=1), col_parts, ((1,), (0,)))
        made = made[:, :128] + made[:, 128:]
        for i in range(8):
            xs[(m * 8 + i) * STEP:(m * 8 + i) * STEP + 64, :] = made[i * 64:(i + 1) * 64]

    for g in range(8):
        beside(g)
        wide = jnp.concatenate([xs[pl.ds(g * 8 + i, 32, stride=STEP), :] for i in range(8)], axis=1)
        wh, wm, wl = split3(wide)
        made = dot(row_parts, jnp.concatenate([wh, wm, wl, wh, wm, wh], axis=0), ((1,), (0,)))
        for i in range(8):
            both = jnp.where(lane < 64, made[:64, i * 128:(i + 1) * 128], made[64:, i * 128:(i + 1) * 128])
            both = both + pltpu.roll(both, 64, 1)
            ts[pl.ds(g * 8 + i, 32, stride=STEP), :] = jnp.where(lane[:32] < 64, both[:32], both[32:])

    for c in range(CHUNKS):
        y = jnp.concatenate([ts[pl.ds(2 * c * STEP, 64), :], ts[pl.ds((2 * c + 1) * STEP, 64), :]], axis=1)
        for part, v in enumerate(split3(y)):
            out_ref[c, part * 64:(part + 1) * 64, :] = v


def sky_kernel(row_s, col_s, count_s, taps_ref, basis_ref, got_ref, obs_hbm, back_hbm, first_ref, second_ref,
               res_hbm, keep_ref, give_ref, taps_pad, bx, bt, b_ref, obs_ref, back_ref, res_ref, sems, ss, xs, xt, acc, near, packed, spots_v, spots_s, listed, sem, *canvases):
    tile = lax.axis_index("sky")
    core = lax.axis_index("epoch") % 2
    lane32 = iota((32, 128), 1)
    late = [pltpu.make_async_copy(obs_hbm, obs_ref, sems.at[0]), pltpu.make_async_copy(back_hbm, back_ref, sems.at[1])]
    for each in late:
        each.start()

    def spots_of(which, there):
        spots = got_ref[which, 48:64, :].astype(F32)
        row = spots.astype(jnp.int32)
        col = 2 * pltpu.roll(spots, 112, 1).astype(jnp.int32) + pltpu.roll(spots, 96, 1).astype(jnp.int32)
        return row, col

    row, col = spots_of(jnp.maximum(tile - 1, 0), None)
    spots_v[0:16, :] = jnp.where((row > 192) & (tile > 0), (row - TR + OFF) * 512 + col, -1)
    row, col = spots_of(jnp.minimum(tile + 1, NSKY - 1), None)
    spots_v[16:32, :] = jnp.where((row < 64) & (tile < NSKY - 1), (row + TR + OFF) * 512 + col, -1)
    copy = pltpu.make_async_copy(spots_v, spots_s, sem)
    copy.start()

    k_at = iota((CAP, 128), 0)
    mine = []
    for o in range(NSKY):
        mine.append(jnp.where(k_at < count_s[0, o], got_ref[o, 16:32, :].astype(F32), 0.0).astype(BF16))
        near[o * 32:o * 32 + 16, :] = got_ref[o, 0:16, :].astype(F32)
        near[o * 32 + 16:o * 32 + 32, :] = got_ref[o, 32:48, :].astype(F32)

    def three(x):
        return jnp.concatenate([x, x[:, :64]], axis=1)

    mine = three(jnp.concatenate(mine, axis=0))
    for j in range(32):
        ss[j * SROWS + SLOTS:(j + 1) * SROWS, :] = jnp.zeros((SROWS - SLOTS, 128), F32)
    copy.wait()

    span = PLANES * CROWS // 8
    counts = [tile * 0]

    def beside(g):
        for canvas in canvases:
            canvas[g * span:(g + 1) * span, :] = jnp.zeros((span, 128), F32)
        count = counts[0]
        for o in (2 * g, 2 * g + 1):
            for which in range(2):
                for k in range(CAP):
                    entry = spots_s[which * 16 + o, k]
                    listed[count] = entry
                    at = o * 32 + which * 16 + k
                    packed[pl.ds(count, 1), :] = near[at:at + 1, :]
                    count = count + jnp.where(entry >= 0, 1, 0)
        counts[0] = count

    convolve(taps_ref, basis_ref, b_ref, taps_pad, bx, bt, beside)
    count = counts[0]

    def render(c, unused):
        made = dot(mine, b_ref[c], ((1,), (0,)))
        made = made.astype(BF16).astype(F32)
        base = pl.multiple_of(c * (2 * SROWS), 8)
        ss[pl.ds(base, OWN), :] = made[:, :128]
        ss[pl.ds(base + SROWS, OWN), :] = made[:, 128:]
        return unused

    lax.fori_loop(0, CHUNKS, render, 0, unroll=4)

    def render_near(b, unused):
        base = pl.multiple_of(b * BLOCK, BLOCK)
        x = three(packed[pl.ds(base, BLOCK), :].astype(BF16))
        for c in range(CHUNKS):
            made = dot(x, b_ref[c], ((1,), (0,))).astype(BF16).astype(F32)
            ss[pl.ds(2 * c * SROWS + OWN + base, BLOCK), :] = made[:, :128]
            ss[pl.ds((2 * c + 1) * SROWS + OWN + base, BLOCK), :] = made[:, 128:]
        return unused

    lax.fori_loop(0, (count + BLOCK - 1) // BLOCK, render_near, 0)

    def put(i, slot, row, col):
        turn = col & 127
        start = (col >> 6) * CROWS + row
        turned = pltpu.roll(ss[pl.ds(slot, 32, stride=SROWS), :], turn, 1)
        inside = ((lane32 - turn) & 127) < 64
        canvases[2 * i][pl.ds(start, 32), :] += jnp.where(inside, turned, 0.0)
        canvases[2 * i + 1][pl.ds(start + 32, 32), :] += jnp.where(inside, 0.0, turned)

    def place(g, unused):
        for i in range(CAP):
            put(i % PAIRS, g * CAP + i, row_s[g, i] + OFF, col_s[g, i])
        return unused

    lax.fori_loop(0, NSKY, place, 0, unroll=4)

    def place_near(g, unused):
        for i in range(GROUP):
            at = g * GROUP + i
            real = at < count
            entry = jnp.where(real, listed[at], OFF * 512)
            put(i % PAIRS, jnp.where(real, OWN + at, SLOTS), entry >> 9, entry & 511)
        return unused

    lax.fori_loop(0, (count + GROUP - 1) // GROUP, place_near, 0)

    for each in late:
        each.wait()

    def pixels(observed, background, image):
        e = jnp.exp(-jnp.abs(image))
        soft = jnp.maximum(image, 0.0) + jnp.log1p(e)
        sig = jnp.where(image >= 0.0, 1.0, e) / (1.0 + e)
        return (observed / (background + soft) - 1.0) * sig

    def images(row, rows):
        left = iota((rows, 128), 1) < 64

        def planes(parity):
            out = []
            for h in range(PLANES):
                at = pl.ds(h * CROWS + OFF + row, rows)
                plane = canvases[parity][at, :]
                for i in range(1, PAIRS):
                    plane = plane + canvases[2 * i + parity][at, :]
                out.append(plane)
            return out

        upper, lower = planes(0), planes(1)
        out = []
        for q in range(4):
            before = jnp.zeros((rows, 128), F32) if q == 0 else upper[2 * q - 1]
            image = upper[2 * q] + jnp.where(left, before, upper[2 * q + 1])
            before = jnp.zeros((rows, 128), F32) if q == 0 else lower[2 * q - 1]
            out.append(image + pltpu.roll(lower[2 * q] + jnp.where(left, lower[2 * q + 1], before), 64, 1))
        return out

    def reach(row, rows, values):
        values = [v.astype(BF16).astype(F32) for v in values]
        turned = [pltpu.roll(v, 64, 1) for v in values]
        left = iota((rows, 128), 1) < 64
        for q in range(4):
            after = min(q + 1, 3)
            even, odd = pl.ds(2 * q * XROWS + row, rows), pl.ds((2 * q + 1) * XROWS + row, rows)
            xs[even, :] = values[q]
            xs[odd, :] = jnp.where(left, values[after], values[q])
            xt[even, :] = turned[q]
            xt[odd, :] = jnp.where(left, turned[q], turned[after])

    def edge(from_first, row, real):
        values = []
        for q, image in enumerate(images(row, 32)):
            lanes = slice(q * 128, (q + 1) * 128)
            observed = jnp.where(from_first, first_ref[:32, lanes], second_ref[:32, lanes])
            background = jnp.where(from_first, first_ref[32:, lanes], second_ref[32:, lanes])
            values.append(jnp.where(real, pixels(observed, background, image), 0.0))
        reach(row, 32, values)

    even = tile % 2 == 0
    edge(jnp.logical_not(even), 0, tile > 0)
    edge(even, 288, tile < NSKY - 1)

    def block(i, unused):
        base = pl.multiple_of(i * 32, 32)
        values = []
        for q, image in enumerate(images(32 + base, 32)):
            lanes = slice(q * 128, (q + 1) * 128)
            r = pixels(obs_ref[pl.ds(base, 32), lanes], back_ref[pl.ds(base, 32), lanes], image)
            res_ref[pl.ds(base, 32), lanes] = r
            values.append(r)
        reach(32 + base, 32, values)
        return unused

    lax.fori_loop(0, 8, block, 0, unroll=8)
    res_copy = pltpu.make_async_copy(res_ref, res_hbm, sems.at[2])
    res_copy.start()

    def window(g, unused):
        for i in range(CAP):
            row, col = row_s[g, i], col_s[g, i]
            turn = col & 127
            start = (col >> 6) * XROWS + row
            inside = ((lane32 - turn) & 127) < 64
            seen = jnp.where(inside, xs[pl.ds(start, 32), :], xt[pl.ds(start + 32, 32), :])
            ss[pl.ds(g * CAP + i, 32, stride=SROWS), :] = pltpu.roll(seen, (128 - turn) & 127, 1)
        return unused

    lax.fori_loop(0, NSKY, window, 0, unroll=4)

    total = jnp.zeros((OWN, 192), F32)
    for c in range(CHUNKS):
        base = 2 * c * SROWS
        w = jnp.concatenate([ss[base:base + OWN, :], ss[base + SROWS:base + SROWS + OWN, :]], axis=1).astype(BF16)
        total = total + dot(w, b_ref[c], ((1,), (1,)))
    grad = total[:, 128:192] + total[:, 64:128] + total[:, :64]
    grad = jnp.concatenate([grad, grad], axis=1)
    for o in range(NSKY):
        acc[o * 16:(o + 1) * 16, :] = jnp.where(k_at < count_s[0, o], grad[o * 16:(o + 1) * 16], 0.0)
    left = iota((4, 128), 1) < 64
    for o in range(NSKY):
        for ref, at in ((keep_ref, o * 16 + core * 8), (give_ref, o * 16 + 8 - core * 8)):
            ref[o] = jnp.where(left, acc[pl.ds(at, 4), :], acc[pl.ds(at + 4, 4), :])
    res_copy.wait()


def owner_kernel(index_s, got_ref, out_ref, first, second, sums):
    core = lax.axis_index("epoch") % 2
    lane = iota((1, 128), 1)
    for t in range(NSKY):
        for r in range(4):
            for hot, k in ((first, r), (second, r + 4)):
                hot[t * 4 + r:t * 4 + r + 1, :] = jnp.where(lane == index_s[t, core * 8 + k], 1.0, 0.0).astype(F32)
    for t in range(NSKY):
        s = got_ref[t * 8]
        for z in range(1, 8):
            s = s + got_ref[t * 8 + z]
        sums[t * 4:(t + 1) * 4, :] = s
    x = sums[...]
    out = dot(x, first[...], ((0,), (0,)), HIGHEST)[:64] + dot(x, second[...], ((0,), (0,)), HIGHEST)[64:]
    out_ref[...] = out


SM = pl.BlockSpec(memory_space=pltpu.SMEM)
HB = pl.BlockSpec(memory_space=pltpu.HBM)
VM = pl.BlockSpec(memory_space=pltpu.VMEM)


def call_send(index, count, params_t, row, col, obs, back):
    return pl.pallas_call(
        send_kernel,
        out_shape=(
            jax.ShapeDtypeStruct((NSKY, 64, 128), BF16),
            jax.ShapeDtypeStruct((64, TW), F32),
            jax.ShapeDtypeStruct((64, TW), F32),
        ),
        in_specs=[SM, SM, VM, VM, VM, HB, HB],
        out_specs=(VM, VM, VM),
        scratch_shapes=[pltpu.VMEM((256, 128), F32), pltpu.SemaphoreType.DMA((4,))],
        compiler_params=pltpu.CompilerParams(vmem_limit_bytes=60 << 20),
    )(index, count, params_t, row, col, obs, back)


def call_sky(row, col, count, taps, basis, got, obs, back, first, second):
    return pl.pallas_call(
        sky_kernel,
        out_shape=(
            jax.ShapeDtypeStruct((TR, TW), F32),
            jax.ShapeDtypeStruct((NSKY, 4, 128), F32),
            jax.ShapeDtypeStruct((NSKY, 4, 128), F32),
        ),
        in_specs=[SM, SM, SM, VM, VM, VM, HB, HB, VM, VM],
        out_specs=(HB, VM, VM),
        scratch_shapes=[
            pltpu.VMEM((8, 128), F32),
            pltpu.VMEM((33 * STEP, 128), F32),
            pltpu.VMEM((33 * STEP, 128), F32),
            pltpu.VMEM((CHUNKS, 192, 256), BF16),
            pltpu.VMEM((TR, TW), F32),
            pltpu.VMEM((TR, TW), F32),
            pltpu.VMEM((TR, TW), F32),
            pltpu.SemaphoreType.DMA((3,)),
            pltpu.VMEM((33 * SROWS, 128), F32),
            pltpu.VMEM((PLANES * XROWS, 128), F32),
            pltpu.VMEM((PLANES * XROWS, 128), F32),
            pltpu.VMEM((OWN, 128), F32),
            pltpu.VMEM((512, 128), F32),
            pltpu.VMEM((520, 128), F32),
            pltpu.VMEM((32, 128), jnp.int32),
            pltpu.SMEM((32, 128), jnp.int32),
            pltpu.SMEM((520,), jnp.int32),
            pltpu.SemaphoreType.DMA,
        ] + [pltpu.VMEM((PLANES * CROWS, 128), F32)] * (2 * PAIRS),
        compiler_params=pltpu.CompilerParams(vmem_limit_bytes=54_000_000),
        cost_estimate=pl.CostEstimate(flops=4 * 10 ** 9, bytes_accessed=4 << 20, transcendentals=0),
    )(row, col, count, taps, basis, got, obs, back, first, second)


def call_owner(index, got):
    return pl.pallas_call(
        owner_kernel,
        out_shape=jax.ShapeDtypeStruct((PS, 128), F32),
        in_specs=[SM, VM],
        out_specs=VM,
        scratch_shapes=[pltpu.VMEM((64, 128), F32)] * 3,
        compiler_params=pltpu.CompilerParams(vmem_limit_bytes=8 << 20),
    )(index, got)


def on_device(params, basis, psf_taps, send_index, tile_count, stamp_row, stamp_col, observed, background):
    n = NSKY
    index = send_index[0]
    row, col = stamp_row[0], stamp_col[0]
    obs, back = observed[0], background[0]
    sent, first, second = call_send(index, tile_count, params.T, row, col, obs, back)
    got = lax.all_to_all(sent, "sky", split_axis=0, concat_axis=0, tiled=True)
    first = lax.ppermute(first, "sky", [(i, i ^ 1) for i in range(n)])
    second = lax.ppermute(second, "sky", [(i, ((i + 1) ^ 1) - 1) for i in range(1, n - 1)])
    residual, keep, give = call_sky(row, col, tile_count, psf_taps[0], basis, got, obs, back, first, second)
    swap = [(i, i ^ 1) for i in range(16)]
    mine = keep + lax.ppermute(give, "epoch", swap)
    spread = jnp.broadcast_to(mine[:, None], (n, 8, 4, 128)).reshape(128, 4, 128)
    groups = [[t * 16 + z * 2 + c for t in range(16) for z in range(8)] for c in range(2)]
    back_home = lax.all_to_all(
        spread, ("sky", "epoch"), split_axis=0, concat_axis=0, tiled=True, axis_index_groups=groups
    )
    part = call_owner(index, back_home)
    grad = part + lax.ppermute(part, "epoch", swap)
    return grad.T, residual[None]


def solution(mesh):
    in_specs = (
        P("sky", None),
        P(),
        P("epoch", None, None),
        P("sky", None, None),
        P("sky", None),
        P("sky", None, None),
        P("sky", None, None),
        P("epoch", "sky", None),
        P("epoch", "sky", None),
    )
    out_specs = (P("sky", None), P("epoch", "sky", None))
    return jax.shard_map(on_device, mesh=mesh, in_specs=in_specs, out_specs=out_specs, check_vma=False)
```

```python
import jax
import jax.numpy as jnp
from jax import lax
from jax.experimental import pallas as pl
from jax.experimental.pallas import tpu as pltpu
from jax.sharding import PartitionSpec as P

PS = 64
TAPS = 51
HALF = 25
TR = 256
TW = 512
CAP = 16
NSKY = 16
OWN = 256
SLOTS = 768
SROWS = 776
OFF = 64
CROWS = 448
XROWS = 320
PLANES = 8
PAIRS = 2
GROUP = 16
CHUNKS = 16
BLOCK = 128
STEP = 72
DEAD = 128
HIGHEST = lax.Precision.HIGHEST
F32 = jnp.float32
BF16 = jnp.bfloat16


def dot(a, b, dims, precision=None):
    return lax.dot_general(a, b, (dims, ((), ())), precision=precision, preferred_element_type=F32)


def split3(x):
    high = x.astype(BF16)
    rest = x - high.astype(F32)
    mid = rest.astype(BF16)
    low = (rest - mid.astype(F32)).astype(BF16)
    return high, mid, low


def iota(shape, axis):
    return lax.broadcasted_iota(jnp.int32, shape, axis)


def send_kernel(index_s, count_s, params_ref, row_ref, col_ref, out_ref, hot):
    lane = iota((1, 128), 1)
    for t in range(NSKY):
        for k in range(CAP):
            hot[t * 16 + k:t * 16 + k + 1, :] = jnp.where(lane == index_s[t, k], 1.0, 0.0).astype(F32)
    rows = dot(hot[...].astype(BF16), params_ref[...], ((1,), (1,)))
    rows = jnp.concatenate([rows, rows], axis=1).astype(BF16)
    none = jnp.zeros((16, 128), BF16)
    owner, k_at = iota((NSKY, CAP), 0), iota((NSKY, CAP), 1)
    count = jnp.zeros((NSKY, CAP), jnp.int32)
    for o in range(NSKY):
        count = jnp.where(owner == o, count_s[0, o], count)
    row = jnp.where(k_at < count, row_ref[...], DEAD)
    col = col_ref[...]
    spots = jnp.concatenate([row, col >> 1, col & 1, jnp.zeros((NSKY, 80), jnp.int32)], axis=1)
    spots = spots.astype(F32).astype(BF16)
    for t in range(NSKY):
        mine = rows[t * 16:(t + 1) * 16]
        out_ref[t, 16:32, :] = mine
        if t + 1 < NSKY:
            out_ref[t + 1, 0:16, :] = mine
        if t > 0:
            out_ref[t - 1, 32:48, :] = mine
        out_ref[t, 48:64, :] = spots
    out_ref[0, 0:16, :] = none
    out_ref[NSKY - 1, 32:48, :] = none


def basis_kernel(taps_ref, basis_ref, out_hbm, taps_pad, xs, ts, out_ref, sems):
    taps_pad[...] = jnp.zeros((8, 128), F32)
    taps = taps_ref[...]
    taps_pad[0:2, 0:TAPS] = taps / jnp.sum(taps, axis=1, keepdims=True)
    lane = iota((64, 128), 1)

    row_taps = jnp.broadcast_to(taps_pad[0:1, :], (32, 128))
    even = pltpu.roll(pltpu.roll(row_taps, 128 - HALF, 1), 0, 1, stride=2, stride_axis=0)
    odd = pltpu.roll(even, 1, 1)
    row_k = jnp.where(lane[:32] < 64, even, pltpu.roll(odd, 64, 1))
    rh, rm, rl = [x.astype(F32) for x in split3(row_k)]
    none = jnp.zeros((64, 128), F32)
    row_parts = jnp.concatenate([rl, rm, rh, rm, rh, rh, none], axis=0).T.astype(BF16)[:, :192]

    col_taps = jnp.broadcast_to(taps_pad[1:2, :], (64, 128))
    col_k = pltpu.roll(pltpu.roll(col_taps, 128 - HALF, 1), 0, 1, stride=1, stride_axis=0)
    col_k = jnp.concatenate([jnp.where(lane < 64, col_k, 0.0), jnp.where(lane < 64, 0.0, pltpu.roll(col_k, 64, 1))], axis=0)
    ch, cm, cl = split3(col_k)
    col_parts = jnp.concatenate([
        jnp.concatenate([ch, cm], axis=1), jnp.concatenate([cl, jnp.zeros((128, 128), BF16)], axis=1)], axis=0)

    for m in range(4):
        x = jnp.concatenate([basis_ref[:, j * 128:(j + 1) * 128] for j in range(m * 8, m * 8 + 8)], axis=0)
        made = dot(jnp.concatenate([x, x], axis=1), col_parts, ((1,), (0,)))
        made = made[:, :128] + made[:, 128:]
        for i in range(8):
            xs[(m * 8 + i) * STEP:(m * 8 + i) * STEP + 64, :] = made[i * 64:(i + 1) * 64]

    for g in range(8):
        wide = jnp.concatenate([xs[pl.ds(g * 8 + i, 32, stride=STEP), :] for i in range(8)], axis=1)
        wh, wm, wl = split3(wide)
        made = dot(row_parts, jnp.concatenate([wh, wm, wl, wh, wm, wh], axis=0), ((1,), (0,)))
        for i in range(8):
            both = jnp.where(lane < 64, made[:64, i * 128:(i + 1) * 128], made[64:, i * 128:(i + 1) * 128])
            both = both + pltpu.roll(both, 64, 1)
            ts[pl.ds(g * 8 + i, 32, stride=STEP), :] = jnp.where(lane[:32] < 64, both[:32], both[32:])

    copies = []
    for c in range(CHUNKS):
        y = jnp.concatenate([ts[pl.ds(2 * c * STEP, 64), :], ts[pl.ds((2 * c + 1) * STEP, 64), :]], axis=1)
        for part, v in enumerate(split3(y)):
            out_ref[c, part * 64:(part + 1) * 64, :] = v
        if c % 4 == 3:
            some = pl.ds(c - 3, 4)
            copies.append(pltpu.make_async_copy(out_ref.at[some], out_hbm.at[some], sems.at[c // 4]))
            copies[-1].start()
    for copy in copies:
        copy.wait()


def sky_kernel(row_s, col_s, count_s, b_hbm, got_ref, obs_hbm, back_hbm, first_ref, second_ref,
               res_hbm, keep_ref, give_ref, b_ref, obs_ref, back_ref, res_ref, sems, ss, xs, xt, acc, near, packed, spots_v, spots_s, listed, sem, *canvases):
    tile = lax.axis_index("sky")
    core = lax.axis_index("epoch") % 2
    lane32 = iota((32, 128), 1)
    b_copy = pltpu.make_async_copy(b_hbm, b_ref, sems.at[3])
    b_copy.start()
    late = [pltpu.make_async_copy(obs_hbm, obs_ref, sems.at[0]), pltpu.make_async_copy(back_hbm, back_ref, sems.at[1])]
    for each in late:
        each.start()

    slot_at = iota((NSKY, 128), 0) * 32 + iota((NSKY, 128), 1)

    def spots_of(peer, slot, shift, inside):
        spots = got_ref[peer, 48:64, :].astype(F32)
        row = spots.astype(jnp.int32)
        col = 2 * pltpu.roll(spots, 112, 1).astype(jnp.int32) + pltpu.roll(spots, 96, 1).astype(jnp.int32)
        return jnp.where(inside(row), (slot * 512 + row + shift) * 512 + col, -1)

    spots_v[0:16, :] = spots_of(
        jnp.maximum(tile - 1, 0), slot_at, OFF - TR, lambda row: (row > 192) & (tile > 0))
    spots_v[16:32, :] = spots_of(
        jnp.minimum(tile + 1, NSKY - 1), slot_at + 16, OFF + TR, lambda row: (row < 64) & (tile < NSKY - 1))
    copy = pltpu.make_async_copy(spots_v, spots_s, sem)
    copy.start()

    k_at = iota((CAP, 128), 0)
    mine = []
    for o in range(NSKY):
        mine.append(jnp.where(k_at < count_s[0, o], got_ref[o, 16:32, :].astype(F32), 0.0).astype(BF16))
        near[o * 32:o * 32 + 16, :] = got_ref[o, 0:16, :].astype(F32)
        near[o * 32 + 16:o * 32 + 32, :] = got_ref[o, 32:48, :].astype(F32)

    def three(x):
        return jnp.concatenate([x, x[:, :64]], axis=1)

    mine = three(jnp.concatenate(mine, axis=0))
    for j in range(32):
        ss[j * SROWS + SLOTS:(j + 1) * SROWS, :] = jnp.zeros((SROWS - SLOTS, 128), F32)
    copy.wait()
    b_copy.wait()

    span = PLANES * CROWS // CHUNKS

    def render(c, count):
        made = dot(mine, b_ref[c], ((1,), (0,)))
        made = made.astype(BF16).astype(F32)
        base = pl.multiple_of(c * (2 * SROWS), 8)
        ss[pl.ds(base, OWN), :] = made[:, :128]
        ss[pl.ds(base + SROWS, OWN), :] = made[:, 128:]
        for canvas in canvases:
            canvas[pl.ds(pl.multiple_of(c * span, 8), span), :] = jnp.zeros((span, 128), F32)
        for which in range(2):
            for k in range(CAP):
                entry = spots_s[which * 16 + c, k]
                listed[count] = entry
                count = count + jnp.where(entry >= 0, 1, 0)
        return count

    count = lax.fori_loop(0, CHUNKS, render, jnp.int32(0), unroll=4)

    def pack(g, unused):
        for i in range(GROUP):
            at = g * GROUP + i
            entry = jnp.where(at < count, listed[at], 0)
            packed[pl.ds(at, 1), :] = near[pl.ds(entry >> 18, 1), :]
        return unused

    lax.fori_loop(0, (count + GROUP - 1) // GROUP, pack, 0)

    def render_near(b, unused):
        base = pl.multiple_of(b * BLOCK, BLOCK)
        x = three(packed[pl.ds(base, BLOCK), :].astype(BF16))
        for c in range(CHUNKS):
            made = dot(x, b_ref[c], ((1,), (0,))).astype(BF16).astype(F32)
            ss[pl.ds(2 * c * SROWS + OWN + base, BLOCK), :] = made[:, :128]
            ss[pl.ds((2 * c + 1) * SROWS + OWN + base, BLOCK), :] = made[:, 128:]
        return unused

    lax.fori_loop(0, (count + BLOCK - 1) // BLOCK, render_near, 0)

    def put(i, slot, row, col):
        turn = col & 127
        start = (col >> 6) * CROWS + row
        turned = pltpu.roll(ss[pl.ds(slot, 32, stride=SROWS), :], turn, 1)
        inside = ((lane32 - turn) & 127) < 64
        canvases[2 * i][pl.ds(start, 32), :] += jnp.where(inside, turned, 0.0)
        canvases[2 * i + 1][pl.ds(start + 32, 32), :] += jnp.where(inside, 0.0, turned)

    def place(g, unused):
        for i in range(CAP):
            put(i % PAIRS, g * CAP + i, row_s[g, i] + OFF, col_s[g, i])
        return unused

    lax.fori_loop(0, NSKY, place, 0, unroll=4)

    def place_near(g, unused):
        for i in range(GROUP):
            at = g * GROUP + i
            real = at < count
            entry = jnp.where(real, listed[at], OFF * 512)
            put(i % PAIRS, jnp.where(real, OWN + at, SLOTS), (entry >> 9) & 511, entry & 511)
        return unused

    lax.fori_loop(0, (count + GROUP - 1) // GROUP, place_near, 0)

    for each in late:
        each.wait()

    def pixels(observed, background, image):
        e = jnp.exp(-jnp.abs(image))
        soft = jnp.maximum(image, 0.0) + jnp.log1p(e)
        sig = jnp.where(image >= 0.0, 1.0, e) / (1.0 + e)
        return (observed / (background + soft) - 1.0) * sig

    def images(row, rows):
        left = iota((rows, 128), 1) < 64

        def planes(parity):
            out = []
            for h in range(PLANES):
                at = pl.ds(h * CROWS + OFF + row, rows)
                plane = canvases[parity][at, :]
                for i in range(1, PAIRS):
                    plane = plane + canvases[2 * i + parity][at, :]
                out.append(plane)
            return out

        upper, lower = planes(0), planes(1)
        out = []
        for q in range(4):
            before = jnp.zeros((rows, 128), F32) if q == 0 else upper[2 * q - 1]
            image = upper[2 * q] + jnp.where(left, before, upper[2 * q + 1])
            before = jnp.zeros((rows, 128), F32) if q == 0 else lower[2 * q - 1]
            out.append(image + pltpu.roll(lower[2 * q] + jnp.where(left, lower[2 * q + 1], before), 64, 1))
        return out

    def reach(row, rows, values):
        values = [v.astype(BF16).astype(F32) for v in values]
        turned = [pltpu.roll(v, 64, 1) for v in values]
        left = iota((rows, 128), 1) < 64
        for q in range(4):
            after = min(q + 1, 3)
            even, odd = pl.ds(2 * q * XROWS + row, rows), pl.ds((2 * q + 1) * XROWS + row, rows)
            xs[even, :] = values[q]
            xs[odd, :] = jnp.where(left, values[after], values[q])
            xt[even, :] = turned[q]
            xt[odd, :] = jnp.where(left, turned[q], turned[after])

    def edge(from_first, row, real):
        values = []
        for q, image in enumerate(images(row, 32)):
            lanes = slice(q * 128, (q + 1) * 128)
            observed = jnp.where(from_first, first_ref[:32, lanes], second_ref[:32, lanes])
            background = jnp.where(from_first, first_ref[32:, lanes], second_ref[32:, lanes])
            values.append(jnp.where(real, pixels(observed, background, image), 0.0))
        reach(row, 32, values)

    even = (tile & 1) == 0
    edge(jnp.logical_not(even), 0, tile > 0)
    edge(even, 288, tile < NSKY - 1)

    def block(i, unused):
        base = pl.multiple_of(i * 32, 32)
        values = []
        for q, image in enumerate(images(32 + base, 32)):
            lanes = slice(q * 128, (q + 1) * 128)
            r = pixels(obs_ref[pl.ds(base, 32), lanes], back_ref[pl.ds(base, 32), lanes], image)
            res_ref[pl.ds(base, 32), lanes] = r
            values.append(r)
        reach(32 + base, 32, values)
        return unused

    lax.fori_loop(0, 8, block, 0, unroll=8)
    res_copy = pltpu.make_async_copy(res_ref, res_hbm, sems.at[2])
    res_copy.start()

    def window(g, unused):
        for i in range(CAP):
            row, col = row_s[g, i], col_s[g, i]
            turn = col & 127
            start = (col >> 6) * XROWS + row
            inside = ((lane32 - turn) & 127) < 64
            seen = jnp.where(inside, xs[pl.ds(start, 32), :], xt[pl.ds(start + 32, 32), :])
            ss[pl.ds(g * CAP + i, 32, stride=SROWS), :] = pltpu.roll(seen, (128 - turn) & 127, 1)
        return unused

    lax.fori_loop(0, NSKY, window, 0, unroll=4)

    total = jnp.zeros((OWN, 192), F32)
    for c in range(CHUNKS):
        base = 2 * c * SROWS
        w = jnp.concatenate([ss[base:base + OWN, :], ss[base + SROWS:base + SROWS + OWN, :]], axis=1).astype(BF16)
        total = total + dot(w, b_ref[c], ((1,), (1,)))
    grad = total[:, 128:192] + total[:, 64:128] + total[:, :64]
    grad = jnp.concatenate([grad, grad], axis=1)
    for o in range(NSKY):
        acc[o * 16:(o + 1) * 16, :] = jnp.where(k_at < count_s[0, o], grad[o * 16:(o + 1) * 16], 0.0)
    left = iota((4, 128), 1) < 64
    for o in range(NSKY):
        for ref, at in ((keep_ref, o * 16 + core * 8), (give_ref, o * 16 + 8 - core * 8)):
            ref[o] = jnp.where(left, acc[pl.ds(at, 4), :], acc[pl.ds(at + 4, 4), :])
    res_copy.wait()


def owner_kernel(index_s, got_ref, out_ref, first, second, sums):
    core = lax.axis_index("epoch") % 2
    lane = iota((1, 128), 1)
    for t in range(NSKY):
        for r in range(4):
            for hot, k in ((first, r), (second, r + 4)):
                hot[t * 4 + r:t * 4 + r + 1, :] = jnp.where(lane == index_s[t, core * 8 + k], 1.0, 0.0).astype(F32)
    for t in range(NSKY):
        s = got_ref[t * 8]
        for z in range(1, 8):
            s = s + got_ref[t * 8 + z]
        sums[t * 4:(t + 1) * 4, :] = s
    x = sums[...]
    out = dot(x, first[...], ((0,), (0,)), HIGHEST)[:64] + dot(x, second[...], ((0,), (0,)), HIGHEST)[64:]
    out_ref[...] = out


SM = pl.BlockSpec(memory_space=pltpu.SMEM)
HB = pl.BlockSpec(memory_space=pltpu.HBM)
VM = pl.BlockSpec(memory_space=pltpu.VMEM)


def call_send(index, count, params_t, row, col):
    return pl.pallas_call(
        send_kernel,
        out_shape=jax.ShapeDtypeStruct((NSKY, 64, 128), BF16),
        in_specs=[SM, SM, VM, VM, VM],
        out_specs=VM,
        scratch_shapes=[pltpu.VMEM((256, 128), F32)],
        compiler_params=pltpu.CompilerParams(vmem_limit_bytes=60 << 20),
        cost_estimate=pl.CostEstimate(flops=8 * 10 ** 9, bytes_accessed=16 << 20, transcendentals=0),
    )(index, count, params_t, row, col)


def call_basis(taps, basis):
    return pl.pallas_call(
        basis_kernel,
        out_shape=jax.ShapeDtypeStruct((CHUNKS, 192, 256), BF16),
        in_specs=[VM, VM],
        out_specs=HB,
        scratch_shapes=[
            pltpu.VMEM((8, 128), F32),
            pltpu.VMEM((33 * STEP, 128), F32),
            pltpu.VMEM((33 * STEP, 128), F32),
            pltpu.VMEM((CHUNKS, 192, 256), BF16),
            pltpu.SemaphoreType.DMA((4,)),
        ],
        compiler_params=pltpu.CompilerParams(vmem_limit_bytes=56_000_000),
        cost_estimate=pl.CostEstimate(flops=10 ** 5, bytes_accessed=1 << 10, transcendentals=0),
    )(taps, basis)


def call_sky(row, col, count, shaped, got, obs, back, first, second):
    return pl.pallas_call(
        sky_kernel,
        out_shape=(
            jax.ShapeDtypeStruct((TR, TW), F32),
            jax.ShapeDtypeStruct((NSKY, 4, 128), F32),
            jax.ShapeDtypeStruct((NSKY, 4, 128), F32),
        ),
        in_specs=[SM, SM, SM, HB, VM, HB, HB, VM, VM],
        out_specs=(HB, VM, VM),
        scratch_shapes=[
            pltpu.VMEM((CHUNKS, 192, 256), BF16),
            pltpu.VMEM((TR, TW), F32),
            pltpu.VMEM((TR, TW), F32),
            pltpu.VMEM((TR, TW), F32),
            pltpu.SemaphoreType.DMA((4,)),
            pltpu.VMEM((33 * SROWS, 128), F32),
            pltpu.VMEM((PLANES * XROWS, 128), F32),
            pltpu.VMEM((PLANES * XROWS, 128), F32),
            pltpu.VMEM((OWN, 128), F32),
            pltpu.VMEM((512, 128), F32),
            pltpu.VMEM((520, 128), F32),
            pltpu.VMEM((32, 128), jnp.int32),
            pltpu.SMEM((32, 128), jnp.int32),
            pltpu.SMEM((520,), jnp.int32),
            pltpu.SemaphoreType.DMA,
        ] + [pltpu.VMEM((PLANES * CROWS, 128), F32)] * (2 * PAIRS),
        compiler_params=pltpu.CompilerParams(vmem_limit_bytes=54_000_000),
        cost_estimate=pl.CostEstimate(flops=4 * 10 ** 9, bytes_accessed=4 << 20, transcendentals=0),
    )(row, col, count, shaped, got, obs, back, first, second)


def call_owner(index, got):
    return pl.pallas_call(
        owner_kernel,
        out_shape=jax.ShapeDtypeStruct((PS, 128), F32),
        in_specs=[SM, VM],
        out_specs=VM,
        scratch_shapes=[pltpu.VMEM((64, 128), F32)] * 3,
        compiler_params=pltpu.CompilerParams(vmem_limit_bytes=8 << 20),
    )(index, got)


def on_device(params, basis, psf_taps, send_index, tile_count, stamp_row, stamp_col, observed, background):
    n = NSKY
    index = send_index[0]
    row, col = stamp_row[0], stamp_col[0]
    obs, back = observed[0], background[0]
    sent = call_send(index, tile_count, params.T, row, col)
    even = (lax.axis_index("sky") & 1) == 0
    low = jnp.concatenate([obs[TR - 32:], back[TR - 32:]], axis=0)
    high = jnp.concatenate([obs[:32], back[:32]], axis=0)
    first, second = jnp.where(even, low, high), jnp.where(even, high, low)
    got = lax.all_to_all(sent, "sky", split_axis=0, concat_axis=0, tiled=True)
    first = lax.ppermute(first, "sky", [(i, i ^ 1) for i in range(n)])
    second = lax.ppermute(second, "sky", [(i, ((i + 1) ^ 1) - 1) for i in range(1, n - 1)])
    residual, keep, give = call_sky(row, col, tile_count, call_basis(psf_taps[0], basis), got, obs, back, first, second)
    swap = [(i, i ^ 1) for i in range(16)]
    mine = keep + lax.ppermute(give, "epoch", swap)
    spread = jnp.broadcast_to(mine[:, None], (n, 8, 4, 128)).reshape(128, 4, 128)
    groups = [[t * 16 + z * 2 + c for t in range(16) for z in range(8)] for c in range(2)]
    back_home = lax.all_to_all(
        spread, ("sky", "epoch"), split_axis=0, concat_axis=0, tiled=True, axis_index_groups=groups
    )
    part = call_owner(index, back_home)
    grad = part + lax.ppermute(part, "epoch", swap)
    return grad.T, residual[None]


def solution(mesh):
    in_specs = (
        P("sky", None),
        P(),
        P("epoch", None, None),
        P("sky", None, None),
        P("sky", None),
        P("sky", None, None),
        P("sky", None, None),
        P("epoch", "sky", None),
        P("epoch", "sky", None),
    )
    out_specs = (P("sky", None), P("epoch", "sky", None))
    return jax.shard_map(on_device, mesh=mesh, in_specs=in_specs, out_specs=out_specs, check_vma=False)
```

```python
import jax
import jax.numpy as jnp
from jax import lax
from jax.experimental import pallas as pl
from jax.experimental.pallas import tpu as pltpu
from jax.sharding import PartitionSpec as P

PS = 64
TAPS = 51
HALF = 25
TR = 256
TW = 512
CAP = 16
NSKY = 16
OWN = 256
SLOTS = 768
SROWS = 776
OFF = 64
CROWS = 448
XROWS = 320
PLANES = 8
PAIRS = 2
GROUP = 16
CHUNKS = 16
BLOCK = 128
STEP = 72
DEAD = 128
HIGHEST = lax.Precision.HIGHEST
F32 = jnp.float32
BF16 = jnp.bfloat16


def dot(a, b, dims, precision=None):
    return lax.dot_general(a, b, (dims, ((), ())), precision=precision, preferred_element_type=F32)


def split3(x):
    high = x.astype(BF16)
    rest = x - high.astype(F32)
    mid = rest.astype(BF16)
    low = (rest - mid.astype(F32)).astype(BF16)
    return high, mid, low


def iota(shape, axis):
    return lax.broadcasted_iota(jnp.int32, shape, axis)


def send_kernel(index_s, count_s, params_ref, row_ref, col_ref, out_ref, hot):
    lane = iota((1, 128), 1)
    for t in range(NSKY):
        for k in range(CAP):
            hot[t * 16 + k:t * 16 + k + 1, :] = jnp.where(lane == index_s[t, k], 1.0, 0.0).astype(F32)
    rows = dot(hot[...].astype(BF16), params_ref[...], ((1,), (1,)))
    rows = jnp.concatenate([rows, rows], axis=1).astype(BF16)
    none = jnp.zeros((16, 128), BF16)
    owner, k_at = iota((NSKY, CAP), 0), iota((NSKY, CAP), 1)
    count = jnp.zeros((NSKY, CAP), jnp.int32)
    for o in range(NSKY):
        count = jnp.where(owner == o, count_s[0, o], count)
    row = jnp.where(k_at < count, row_ref[...], DEAD)
    col = col_ref[...]
    spots = jnp.concatenate([row, col >> 1, col & 1, jnp.zeros((NSKY, 80), jnp.int32)], axis=1)
    spots = spots.astype(F32).astype(BF16)
    for t in range(NSKY):
        mine = rows[t * 16:(t + 1) * 16]
        out_ref[t, 16:32, :] = mine
        if t + 1 < NSKY:
            out_ref[t + 1, 0:16, :] = mine
        if t > 0:
            out_ref[t - 1, 32:48, :] = mine
        out_ref[t, 48:64, :] = spots
    out_ref[0, 0:16, :] = none
    out_ref[NSKY - 1, 32:48, :] = none


def basis_kernel(index_s, taps_ref, basis_ref, out_hbm, first, second, taps_pad, xs, ts, out_ref, sems):
    core = lax.axis_index("epoch") & 1
    source = iota((1, 128), 1)
    for t in range(NSKY):
        for r in range(4):
            for hot, k in ((first, r), (second, r + 4)):
                hot[t * 4 + r:t * 4 + r + 1, :] = jnp.where(source == index_s[t, core * 8 + k], 1.0, 0.0).astype(F32)
    taps_pad[...] = jnp.zeros((8, 128), F32)
    taps = taps_ref[...]
    taps_pad[0:2, 0:TAPS] = taps / jnp.sum(taps, axis=1, keepdims=True)
    lane = iota((64, 128), 1)

    row_taps = jnp.broadcast_to(taps_pad[0:1, :], (32, 128))
    even = pltpu.roll(pltpu.roll(row_taps, 128 - HALF, 1), 0, 1, stride=2, stride_axis=0)
    odd = pltpu.roll(even, 1, 1)
    row_k = jnp.where(lane[:32] < 64, even, pltpu.roll(odd, 64, 1))
    rh, rm, rl = [x.astype(F32) for x in split3(row_k)]
    none = jnp.zeros((64, 128), F32)
    row_parts = jnp.concatenate([rl, rm, rh, rm, rh, rh, none], axis=0).T.astype(BF16)[:, :192]

    col_taps = jnp.broadcast_to(taps_pad[1:2, :], (64, 128))
    col_k = pltpu.roll(pltpu.roll(col_taps, 128 - HALF, 1), 0, 1, stride=1, stride_axis=0)
    col_k = jnp.concatenate([jnp.where(lane < 64, col_k, 0.0), jnp.where(lane < 64, 0.0, pltpu.roll(col_k, 64, 1))], axis=0)
    ch, cm, cl = split3(col_k)
    col_parts = jnp.concatenate([
        jnp.concatenate([ch, cm], axis=1), jnp.concatenate([cl, jnp.zeros((128, 128), BF16)], axis=1)], axis=0)

    for m in range(4):
        x = jnp.concatenate([basis_ref[:, j * 128:(j + 1) * 128] for j in range(m * 8, m * 8 + 8)], axis=0)
        made = dot(jnp.concatenate([x, x], axis=1), col_parts, ((1,), (0,)))
        made = made[:, :128] + made[:, 128:]
        for i in range(8):
            xs[(m * 8 + i) * STEP:(m * 8 + i) * STEP + 64, :] = made[i * 64:(i + 1) * 64]

    for g in range(8):
        wide = jnp.concatenate([xs[pl.ds(g * 8 + i, 32, stride=STEP), :] for i in range(8)], axis=1)
        wh, wm, wl = split3(wide)
        made = dot(row_parts, jnp.concatenate([wh, wm, wl, wh, wm, wh], axis=0), ((1,), (0,)))
        for i in range(8):
            both = jnp.where(lane < 64, made[:64, i * 128:(i + 1) * 128], made[64:, i * 128:(i + 1) * 128])
            both = both + pltpu.roll(both, 64, 1)
            ts[pl.ds(g * 8 + i, 32, stride=STEP), :] = jnp.where(lane[:32] < 64, both[:32], both[32:])

    copies = []
    for c in range(CHUNKS):
        y = jnp.concatenate([ts[pl.ds(2 * c * STEP, 64), :], ts[pl.ds((2 * c + 1) * STEP, 64), :]], axis=1)
        for part, v in enumerate(split3(y)):
            out_ref[c, part * 64:(part + 1) * 64, :] = v
        if c % 4 == 3:
            some = pl.ds(c - 3, 4)
            copies.append(pltpu.make_async_copy(out_ref.at[some], out_hbm.at[some], sems.at[c // 4]))
            copies[-1].start()
    for copy in copies:
        copy.wait()


def sky_kernel(row_s, col_s, count_s, b_hbm, got_ref, obs_hbm, back_hbm, first_ref, second_ref,
               res_hbm, keep_ref, give_ref, b_ref, obs_ref, back_ref, res_ref, sems, ss, xs, xt, acc, near, packed, spots_v, spots_s, listed, sem, *canvases):
    tile = lax.axis_index("sky")
    core = lax.axis_index("epoch") % 2
    lane32 = iota((32, 128), 1)

    def b_copy(i):
        some = pl.ds(4 * i, 4)
        return pltpu.make_async_copy(b_hbm.at[some], b_ref.at[some], sems.at[3 + i])

    for i in range(4):
        b_copy(i).start()
    late = [pltpu.make_async_copy(obs_hbm, obs_ref, sems.at[0]), pltpu.make_async_copy(back_hbm, back_ref, sems.at[1])]
    for each in late:
        each.start()

    slot_at = iota((NSKY, 128), 0) * 32 + iota((NSKY, 128), 1)

    def spots_of(peer, slot, shift, inside):
        spots = got_ref[peer, 48:64, :].astype(F32)
        row = spots.astype(jnp.int32)
        col = 2 * pltpu.roll(spots, 112, 1).astype(jnp.int32) + pltpu.roll(spots, 96, 1).astype(jnp.int32)
        return jnp.where(inside(row), (slot * 512 + row + shift) * 512 + col, -1)

    spots_v[0:16, :] = spots_of(
        jnp.maximum(tile - 1, 0), slot_at, OFF - TR, lambda row: (row > 192) & (tile > 0))
    spots_v[16:32, :] = spots_of(
        jnp.minimum(tile + 1, NSKY - 1), slot_at + 16, OFF + TR, lambda row: (row < 64) & (tile < NSKY - 1))
    copy = pltpu.make_async_copy(spots_v, spots_s, sem)
    copy.start()

    k_at = iota((CAP, 128), 0)
    mine = []
    for o in range(NSKY):
        mine.append(jnp.where(k_at < count_s[0, o], got_ref[o, 16:32, :].astype(F32), 0.0).astype(BF16))
        near[o * 32:o * 32 + 16, :] = got_ref[o, 0:16, :].astype(F32)
        near[o * 32 + 16:o * 32 + 32, :] = got_ref[o, 32:48, :].astype(F32)

    def three(x):
        return jnp.concatenate([x, x[:, :64]], axis=1)

    mine = three(jnp.concatenate(mine, axis=0))
    for j in range(32):
        ss[j * SROWS + SLOTS:(j + 1) * SROWS, :] = jnp.zeros((SROWS - SLOTS, 128), F32)
    copy.wait()

    span = PLANES * CROWS // CHUNKS

    def render(c, count):
        made = dot(mine, b_ref[c], ((1,), (0,)))
        made = made.astype(BF16).astype(F32)
        base = pl.multiple_of(c * (2 * SROWS), 8)
        ss[pl.ds(base, OWN), :] = made[:, :128]
        ss[pl.ds(base + SROWS, OWN), :] = made[:, 128:]
        for canvas in canvases:
            canvas[pl.ds(pl.multiple_of(c * span, 8), span), :] = jnp.zeros((span, 128), F32)
        for which in range(2):
            for k in range(CAP):
                entry = spots_s[which * 16 + c, k]
                listed[count] = entry
                count = count + jnp.where(entry >= 0, 1, 0)
        return count

    count = tile * 0
    for i in range(4):
        b_copy(i).wait()
        count = lax.fori_loop(4 * i, 4 * i + 4, render, count, unroll=4)

    def pack(g, unused):
        for i in range(GROUP):
            at = g * GROUP + i
            entry = jnp.where(at < count, listed[at], 0)
            packed[pl.ds(at, 1), :] = near[pl.ds(entry >> 18, 1), :]
        return unused

    lax.fori_loop(0, (count + GROUP - 1) // GROUP, pack, 0)

    def render_near(b, unused):
        base = pl.multiple_of(b * BLOCK, BLOCK)
        x = three(packed[pl.ds(base, BLOCK), :].astype(BF16))
        for c in range(CHUNKS):
            made = dot(x, b_ref[c], ((1,), (0,))).astype(BF16).astype(F32)
            ss[pl.ds(2 * c * SROWS + OWN + base, BLOCK), :] = made[:, :128]
            ss[pl.ds((2 * c + 1) * SROWS + OWN + base, BLOCK), :] = made[:, 128:]
        return unused

    lax.fori_loop(0, (count + BLOCK - 1) // BLOCK, render_near, 0)

    def put(i, slot, row, col):
        turn = col & 127
        start = (col >> 6) * CROWS + row
        turned = pltpu.roll(ss[pl.ds(slot, 32, stride=SROWS), :], turn, 1)
        inside = ((lane32 - turn) & 127) < 64
        canvases[2 * i][pl.ds(start, 32), :] += jnp.where(inside, turned, 0.0)
        canvases[2 * i + 1][pl.ds(start + 32, 32), :] += jnp.where(inside, 0.0, turned)

    def place(g, unused):
        for i in range(CAP):
            put(i % PAIRS, g * CAP + i, row_s[g, i] + OFF, col_s[g, i])
        return unused

    lax.fori_loop(0, NSKY, place, 0, unroll=4)

    def place_near(g, unused):
        for i in range(GROUP):
            at = g * GROUP + i
            real = at < count
            entry = jnp.where(real, listed[at], OFF * 512)
            put(i % PAIRS, jnp.where(real, OWN + at, SLOTS), (entry >> 9) & 511, entry & 511)
        return unused

    lax.fori_loop(0, (count + GROUP - 1) // GROUP, place_near, 0)

    for each in late:
        each.wait()

    def pixels(observed, background, image):
        e = jnp.exp(-jnp.abs(image))
        soft = jnp.maximum(image, 0.0) + jnp.log1p(e)
        sig = jnp.where(image >= 0.0, 1.0, e) / (1.0 + e)
        return (observed / (background + soft) - 1.0) * sig

    def images(row, rows):
        left = iota((rows, 128), 1) < 64

        def planes(parity):
            out = []
            for h in range(PLANES):
                at = pl.ds(h * CROWS + OFF + row, rows)
                plane = canvases[parity][at, :]
                for i in range(1, PAIRS):
                    plane = plane + canvases[2 * i + parity][at, :]
                out.append(plane)
            return out

        upper, lower = planes(0), planes(1)
        out = []
        for q in range(4):
            before = jnp.zeros((rows, 128), F32) if q == 0 else upper[2 * q - 1]
            image = upper[2 * q] + jnp.where(left, before, upper[2 * q + 1])
            before = jnp.zeros((rows, 128), F32) if q == 0 else lower[2 * q - 1]
            out.append(image + pltpu.roll(lower[2 * q] + jnp.where(left, lower[2 * q + 1], before), 64, 1))
        return out

    def reach(row, rows, values):
        values = [v.astype(BF16).astype(F32) for v in values]
        turned = [pltpu.roll(v, 64, 1) for v in values]
        left = iota((rows, 128), 1) < 64
        for q in range(4):
            after = min(q + 1, 3)
            even, odd = pl.ds(2 * q * XROWS + row, rows), pl.ds((2 * q + 1) * XROWS + row, rows)
            xs[even, :] = values[q]
            xs[odd, :] = jnp.where(left, values[after], values[q])
            xt[even, :] = turned[q]
            xt[odd, :] = jnp.where(left, turned[q], turned[after])

    def edge(from_first, row, real):
        values = []
        for q, image in enumerate(images(row, 32)):
            lanes = slice(q * 128, (q + 1) * 128)
            observed = jnp.where(from_first, first_ref[:32, lanes], second_ref[:32, lanes])
            background = jnp.where(from_first, first_ref[32:, lanes], second_ref[32:, lanes])
            values.append(jnp.where(real, pixels(observed, background, image), 0.0))
        reach(row, 32, values)

    even = (tile & 1) == 0
    edge(jnp.logical_not(even), 0, tile > 0)
    edge(even, 288, tile < NSKY - 1)

    def block(i, unused):
        base = pl.multiple_of(i * 32, 32)
        values = []
        for q, image in enumerate(images(32 + base, 32)):
            lanes = slice(q * 128, (q + 1) * 128)
            r = pixels(obs_ref[pl.ds(base, 32), lanes], back_ref[pl.ds(base, 32), lanes], image)
            res_ref[pl.ds(base, 32), lanes] = r
            values.append(r)
        reach(32 + base, 32, values)
        return unused

    lax.fori_loop(0, 8, block, 0, unroll=8)
    res_copy = pltpu.make_async_copy(res_ref, res_hbm, sems.at[2])
    res_copy.start()

    def window(g, unused):
        for i in range(CAP):
            row, col = row_s[g, i], col_s[g, i]
            turn = col & 127
            start = (col >> 6) * XROWS + row
            inside = ((lane32 - turn) & 127) < 64
            seen = jnp.where(inside, xs[pl.ds(start, 32), :], xt[pl.ds(start + 32, 32), :])
            ss[pl.ds(g * CAP + i, 32, stride=SROWS), :] = pltpu.roll(seen, (128 - turn) & 127, 1)
        return unused

    lax.fori_loop(0, NSKY, window, 0, unroll=4)

    total = jnp.zeros((OWN, 192), F32)
    for c in range(CHUNKS):
        base = 2 * c * SROWS
        w = jnp.concatenate([ss[base:base + OWN, :], ss[base + SROWS:base + SROWS + OWN, :]], axis=1).astype(BF16)
        total = total + dot(w, b_ref[c], ((1,), (1,)))
    grad = total[:, 128:192] + total[:, 64:128] + total[:, :64]
    grad = jnp.concatenate([grad, grad], axis=1)
    for o in range(NSKY):
        acc[o * 16:(o + 1) * 16, :] = jnp.where(k_at < count_s[0, o], grad[o * 16:(o + 1) * 16], 0.0)
    left = iota((4, 128), 1) < 64
    for o in range(NSKY):
        for ref, at in ((keep_ref, o * 16 + core * 8), (give_ref, o * 16 + 8 - core * 8)):
            ref[o] = jnp.where(left, acc[pl.ds(at, 4), :], acc[pl.ds(at + 4, 4), :])
    res_copy.wait()


def owner_kernel(first, second, got_ref, out_ref, sums):
    for t in range(NSKY):
        s = got_ref[t * 8]
        for z in range(1, 8):
            s = s + got_ref[t * 8 + z]
        sums[t * 4:(t + 1) * 4, :] = s
    x = sums[...]
    out = dot(x, first[...], ((0,), (0,)), HIGHEST)[:64] + dot(x, second[...], ((0,), (0,)), HIGHEST)[64:]
    out_ref[...] = out


SM = pl.BlockSpec(memory_space=pltpu.SMEM)
HB = pl.BlockSpec(memory_space=pltpu.HBM)
VM = pl.BlockSpec(memory_space=pltpu.VMEM)


def call_send(index, count, params_t, row, col):
    return pl.pallas_call(
        send_kernel,
        out_shape=jax.ShapeDtypeStruct((NSKY, 64, 128), BF16),
        in_specs=[SM, SM, VM, VM, VM],
        out_specs=VM,
        scratch_shapes=[pltpu.VMEM((256, 128), F32)],
        compiler_params=pltpu.CompilerParams(vmem_limit_bytes=60 << 20),
        cost_estimate=pl.CostEstimate(flops=8 * 10 ** 9, bytes_accessed=16 << 20, transcendentals=0),
    )(index, count, params_t, row, col)


def call_basis(index, taps, basis):
    return pl.pallas_call(
        basis_kernel,
        out_shape=(
            jax.ShapeDtypeStruct((CHUNKS, 192, 256), BF16),
            jax.ShapeDtypeStruct((64, 128), F32),
            jax.ShapeDtypeStruct((64, 128), F32),
        ),
        in_specs=[SM, VM, VM],
        out_specs=(HB, VM, VM),
        scratch_shapes=[
            pltpu.VMEM((8, 128), F32),
            pltpu.VMEM((33 * STEP, 128), F32),
            pltpu.VMEM((33 * STEP, 128), F32),
            pltpu.VMEM((CHUNKS, 192, 256), BF16),
            pltpu.SemaphoreType.DMA((4,)),
        ],
        compiler_params=pltpu.CompilerParams(vmem_limit_bytes=55_000_000),
        cost_estimate=pl.CostEstimate(flops=10 ** 5, bytes_accessed=1 << 10, transcendentals=0),
    )(index, taps, basis)


def call_sky(row, col, count, shaped, got, obs, back, first, second):
    return pl.pallas_call(
        sky_kernel,
        out_shape=(
            jax.ShapeDtypeStruct((TR, TW), F32),
            jax.ShapeDtypeStruct((NSKY, 4, 128), F32),
            jax.ShapeDtypeStruct((NSKY, 4, 128), F32),
        ),
        in_specs=[SM, SM, SM, HB, VM, HB, HB, VM, VM],
        out_specs=(HB, VM, VM),
        scratch_shapes=[
            pltpu.VMEM((CHUNKS, 192, 256), BF16),
            pltpu.VMEM((TR, TW), F32),
            pltpu.VMEM((TR, TW), F32),
            pltpu.VMEM((TR, TW), F32),
            pltpu.SemaphoreType.DMA((7,)),
            pltpu.VMEM((33 * SROWS, 128), F32),
            pltpu.VMEM((PLANES * XROWS, 128), F32),
            pltpu.VMEM((PLANES * XROWS, 128), F32),
            pltpu.VMEM((OWN, 128), F32),
            pltpu.VMEM((512, 128), F32),
            pltpu.VMEM((520, 128), F32),
            pltpu.VMEM((32, 128), jnp.int32),
            pltpu.SMEM((32, 128), jnp.int32),
            pltpu.SMEM((520,), jnp.int32),
            pltpu.SemaphoreType.DMA,
        ] + [pltpu.VMEM((PLANES * CROWS, 128), F32)] * (2 * PAIRS),
        compiler_params=pltpu.CompilerParams(vmem_limit_bytes=54_000_000),
        cost_estimate=pl.CostEstimate(flops=4 * 10 ** 9, bytes_accessed=4 << 20, transcendentals=0),
    )(row, col, count, shaped, got, obs, back, first, second)


def call_owner(first, second, got):
    return pl.pallas_call(
        owner_kernel,
        out_shape=jax.ShapeDtypeStruct((PS, 128), F32),
        in_specs=[VM, VM, VM],
        out_specs=VM,
        scratch_shapes=[pltpu.VMEM((64, 128), F32)],
        compiler_params=pltpu.CompilerParams(vmem_limit_bytes=8 << 20),
    )(first, second, got)


def on_device(params, basis, psf_taps, send_index, tile_count, stamp_row, stamp_col, observed, background):
    n = NSKY
    index = send_index[0]
    row, col = stamp_row[0], stamp_col[0]
    obs, back = observed[0], background[0]
    sent = call_send(index, tile_count, params.T, row, col)
    even = (lax.axis_index("sky") & 1) == 0
    low = jnp.concatenate([obs[TR - 32:], back[TR - 32:]], axis=0)
    high = jnp.concatenate([obs[:32], back[:32]], axis=0)
    first, second = jnp.where(even, low, high), jnp.where(even, high, low)
    got = lax.all_to_all(sent, "sky", split_axis=0, concat_axis=0, tiled=True)
    first = lax.ppermute(first, "sky", [(i, i ^ 1) for i in range(n)])
    second = lax.ppermute(second, "sky", [(i, ((i + 1) ^ 1) - 1) for i in range(1, n - 1)])
    shaped, hot_first, hot_second = call_basis(index, psf_taps[0], basis)
    residual, keep, give = call_sky(row, col, tile_count, shaped, got, obs, back, first, second)
    swap = [(i, i ^ 1) for i in range(16)]
    mine = keep + lax.ppermute(give, "epoch", swap)
    spread = jnp.broadcast_to(mine[:, None], (n, 8, 4, 128)).reshape(128, 4, 128)
    groups = [[t * 16 + z * 2 + c for t in range(16) for z in range(8)] for c in range(2)]
    back_home = lax.all_to_all(
        spread, ("sky", "epoch"), split_axis=0, concat_axis=0, tiled=True, axis_index_groups=groups
    )
    part = call_owner(hot_first, hot_second, back_home)
    grad = part + lax.ppermute(part, "epoch", swap)
    return grad.T, residual[None]


def solution(mesh):
    in_specs = (
        P("sky", None),
        P(),
        P("epoch", None, None),
        P("sky", None, None),
        P("sky", None),
        P("sky", None, None),
        P("sky", None, None),
        P("epoch", "sky", None),
        P("epoch", "sky", None),
    )
    out_specs = (P("sky", None), P("epoch", "sky", None))
    return jax.shard_map(on_device, mesh=mesh, in_specs=in_specs, out_specs=out_specs, check_vma=False)
```

```python
import jax
import jax.numpy as jnp
from jax import lax
from jax.experimental import pallas as pl
from jax.experimental.pallas import tpu as pltpu
from jax.sharding import PartitionSpec as P

PS = 64
TAPS = 51
HALF = 25
TR = 256
TW = 512
CAP = 16
NSKY = 16
OWN = 256
SLOTS = 768
SROWS = 776
OFF = 64
CROWS = 448
XROWS = 320
PLANES = 8
PAIRS = 2
GROUP = 16
CHUNKS = 16
BLOCK = 128
STEP = 72
DEAD = 128
HIGHEST = lax.Precision.HIGHEST
F32 = jnp.float32
BF16 = jnp.bfloat16


def dot(a, b, dims, precision=None):
    return lax.dot_general(a, b, (dims, ((), ())), precision=precision, preferred_element_type=F32)


def split3(x):
    high = x.astype(BF16)
    rest = x - high.astype(F32)
    mid = rest.astype(BF16)
    low = (rest - mid.astype(F32)).astype(BF16)
    return high, mid, low


def iota(shape, axis):
    return lax.broadcasted_iota(jnp.int32, shape, axis)


def send_kernel(index_s, count_s, params_ref, row_ref, col_ref, out_ref, hot):
    lane = iota((1, 128), 1)
    for t in range(NSKY):
        for k in range(CAP):
            hot[t * 16 + k:t * 16 + k + 1, :] = jnp.where(lane == index_s[t, k], 1.0, 0.0).astype(F32)
    rows = dot(hot[...].astype(BF16), params_ref[...], ((1,), (1,)))
    rows = jnp.concatenate([rows, rows], axis=1).astype(BF16)
    none = jnp.zeros((16, 128), BF16)
    owner, k_at = iota((NSKY, CAP), 0), iota((NSKY, CAP), 1)
    count = jnp.zeros((NSKY, CAP), jnp.int32)
    for o in range(NSKY):
        count = jnp.where(owner == o, count_s[0, o], count)
    row = jnp.where(k_at < count, row_ref[...], DEAD)
    col = col_ref[...]
    spots = jnp.concatenate([row, col >> 1, col & 1, jnp.zeros((NSKY, 80), jnp.int32)], axis=1)
    spots = spots.astype(F32).astype(BF16)
    for t in range(NSKY):
        mine = rows[t * 16:(t + 1) * 16]
        out_ref[t, 16:32, :] = mine
        if t + 1 < NSKY:
            out_ref[t + 1, 0:16, :] = mine
        if t > 0:
            out_ref[t - 1, 32:48, :] = mine
        out_ref[t, 48:64, :] = spots
    out_ref[0, 0:16, :] = none
    out_ref[NSKY - 1, 32:48, :] = none


def basis_kernel(index_s, taps_ref, basis_ref, out_hbm, first, second, taps_pad, xs, ts, out_ref, sems):
    core = lax.axis_index("epoch") & 1
    source = iota((1, 128), 1)
    for t in range(NSKY):
        for r in range(4):
            for hot, k in ((first, r), (second, r + 4)):
                hot[t * 4 + r:t * 4 + r + 1, :] = jnp.where(source == index_s[t, core * 8 + k], 1.0, 0.0).astype(F32)
    taps_pad[...] = jnp.zeros((8, 128), F32)
    taps = taps_ref[...]
    taps_pad[0:2, 0:TAPS] = taps / jnp.sum(taps, axis=1, keepdims=True)
    lane = iota((64, 128), 1)

    row_taps = jnp.broadcast_to(taps_pad[0:1, :], (32, 128))
    even = pltpu.roll(pltpu.roll(row_taps, 128 - HALF, 1), 0, 1, stride=2, stride_axis=0)
    odd = pltpu.roll(even, 1, 1)
    row_k = jnp.where(lane[:32] < 64, even, pltpu.roll(odd, 64, 1))
    rh, rm, rl = [x.astype(F32) for x in split3(row_k)]
    none = jnp.zeros((64, 128), F32)
    row_parts = jnp.concatenate([rl, rm, rh, rm, rh, rh, none], axis=0).T.astype(BF16)[:, :192]

    col_taps = jnp.broadcast_to(taps_pad[1:2, :], (64, 128))
    col_k = pltpu.roll(pltpu.roll(col_taps, 128 - HALF, 1), 0, 1, stride=1, stride_axis=0)
    col_k = jnp.concatenate([jnp.where(lane < 64, col_k, 0.0), jnp.where(lane < 64, 0.0, pltpu.roll(col_k, 64, 1))], axis=0)
    ch, cm, cl = split3(col_k)
    col_parts = jnp.concatenate([
        jnp.concatenate([ch, cm], axis=1), jnp.concatenate([cl, jnp.zeros((128, 128), BF16)], axis=1)], axis=0)

    for m in range(4):
        x = jnp.concatenate([basis_ref[:, j * 128:(j + 1) * 128] for j in range(m * 8, m * 8 + 8)], axis=0)
        made = dot(jnp.concatenate([x, x], axis=1), col_parts, ((1,), (0,)))
        made = made[:, :128] + made[:, 128:]
        for i in range(8):
            xs[(m * 8 + i) * STEP:(m * 8 + i) * STEP + 64, :] = made[i * 64:(i + 1) * 64]

    for g in range(8):
        wide = jnp.concatenate([xs[pl.ds(g * 8 + i, 32, stride=STEP), :] for i in range(8)], axis=1)
        wh, wm, wl = split3(wide)
        made = dot(row_parts, jnp.concatenate([wh, wm, wl, wh, wm, wh], axis=0), ((1,), (0,)))
        for i in range(8):
            both = jnp.where(lane < 64, made[:64, i * 128:(i + 1) * 128], made[64:, i * 128:(i + 1) * 128])
            both = both + pltpu.roll(both, 64, 1)
            ts[pl.ds(g * 8 + i, 32, stride=STEP), :] = jnp.where(lane[:32] < 64, both[:32], both[32:])

    copies = []
    for c in range(CHUNKS):
        y = jnp.concatenate([ts[pl.ds(2 * c * STEP, 64), :], ts[pl.ds((2 * c + 1) * STEP, 64), :]], axis=1)
        for part, v in enumerate(split3(y)):
            out_ref[c, part * 64:(part + 1) * 64, :] = v
        if c % 4 == 3:
            some = pl.ds(c - 3, 4)
            copies.append(pltpu.make_async_copy(out_ref.at[some], out_hbm.at[some], sems.at[c // 4]))
            copies[-1].start()
    for copy in copies:
        copy.wait()


def sky_kernel(row_s, col_s, count_s, b_hbm, got_ref, obs_hbm, back_hbm, first_ref, second_ref,
               res_hbm, keep_ref, give_ref, b_ref, obs_ref, back_ref, res_ref, sems, ss, xs, xt, acc, near, packed, spots_v, spots_s, listed, sem, *canvases):
    tile = lax.axis_index("sky")
    core = lax.axis_index("epoch") % 2
    lane32 = iota((32, 128), 1)

    def b_copy(i):
        some = pl.ds(4 * i, 4)
        return pltpu.make_async_copy(b_hbm.at[some], b_ref.at[some], sems.at[3 + i])

    for i in range(4):
        b_copy(i).start()
    late = [pltpu.make_async_copy(obs_hbm, obs_ref, sems.at[0]), pltpu.make_async_copy(back_hbm, back_ref, sems.at[1])]
    for each in late:
        each.start()

    slot_at = iota((NSKY, 128), 0) * 32 + iota((NSKY, 128), 1)

    def spots_of(peer, slot, shift, inside):
        spots = got_ref[peer, 48:64, :].astype(F32)
        row = spots.astype(jnp.int32)
        col = 2 * pltpu.roll(spots, 112, 1).astype(jnp.int32) + pltpu.roll(spots, 96, 1).astype(jnp.int32)
        return jnp.where(inside(row), (slot * 512 + row + shift) * 512 + col, -1)

    spots_v[0:16, :] = spots_of(
        jnp.maximum(tile - 1, 0), slot_at, OFF - TR, lambda row: (row > 192) & (tile > 0))
    spots_v[16:32, :] = spots_of(
        jnp.minimum(tile + 1, NSKY - 1), slot_at + 16, OFF + TR, lambda row: (row < 64) & (tile < NSKY - 1))
    copy = pltpu.make_async_copy(spots_v, spots_s, sem)
    copy.start()

    k_at = iota((CAP, 128), 0)
    mine = []
    for o in range(NSKY):
        mine.append(jnp.where(k_at < count_s[0, o], got_ref[o, 16:32, :].astype(F32), 0.0).astype(BF16))
        near[o * 32:o * 32 + 16, :] = got_ref[o, 0:16, :].astype(F32)
        near[o * 32 + 16:o * 32 + 32, :] = got_ref[o, 32:48, :].astype(F32)

    def three(x):
        return jnp.concatenate([x, x[:, :64]], axis=1)

    mine = three(jnp.concatenate(mine, axis=0))
    for j in range(32):
        ss[j * SROWS + SLOTS:(j + 1) * SROWS, :] = jnp.zeros((SROWS - SLOTS, 128), F32)
    copy.wait()

    span = PLANES * CROWS // CHUNKS

    def render(c, count):
        made = dot(mine, b_ref[c], ((1,), (0,)))
        made = made.astype(BF16).astype(F32)
        base = pl.multiple_of(c * (2 * SROWS), 8)
        ss[pl.ds(base, OWN), :] = made[:, :128]
        ss[pl.ds(base + SROWS, OWN), :] = made[:, 128:]
        for canvas in canvases:
            canvas[pl.ds(pl.multiple_of(c * span, 8), span), :] = jnp.zeros((span, 128), F32)
        for which in range(2):
            for k in range(CAP):
                entry = spots_s[which * 16 + c, k]
                listed[count] = entry
                count = count + jnp.where(entry >= 0, 1, 0)
        return count

    count = tile * 0
    for i in range(4):
        b_copy(i).wait()
        count = lax.fori_loop(4 * i, 4 * i + 4, render, count, unroll=4)

    def pack(g, unused):
        for i in range(GROUP):
            at = g * GROUP + i
            entry = jnp.where(at < count, listed[at], 0)
            packed[pl.ds(at, 1), :] = near[pl.ds(entry >> 18, 1), :]
        return unused

    lax.fori_loop(0, (count + GROUP - 1) // GROUP, pack, 0)

    def render_near(b, unused):
        base = pl.multiple_of(b * BLOCK, BLOCK)
        x = three(packed[pl.ds(base, BLOCK), :].astype(BF16))
        for c in range(CHUNKS):
            made = dot(x, b_ref[c], ((1,), (0,))).astype(BF16).astype(F32)
            ss[pl.ds(2 * c * SROWS + OWN + base, BLOCK), :] = made[:, :128]
            ss[pl.ds((2 * c + 1) * SROWS + OWN + base, BLOCK), :] = made[:, 128:]
        return unused

    lax.fori_loop(0, (count + BLOCK - 1) // BLOCK, render_near, 0)

    def put(i, slot, row, col):
        turn = col & 127
        start = (col >> 6) * CROWS + row
        turned = pltpu.roll(ss[pl.ds(slot, 32, stride=SROWS), :], turn, 1)
        inside = ((lane32 - turn) & 127) < 64
        canvases[2 * i][pl.ds(start, 32), :] += jnp.where(inside, turned, 0.0)
        canvases[2 * i + 1][pl.ds(start + 32, 32), :] += jnp.where(inside, 0.0, turned)

    def place(g, unused):
        for i in range(CAP):
            put(i % PAIRS, g * CAP + i, row_s[g, i] + OFF, col_s[g, i])
        return unused

    lax.fori_loop(0, NSKY, place, 0, unroll=16)

    def place_near(g, unused):
        for i in range(GROUP):
            at = g * GROUP + i
            real = at < count
            entry = jnp.where(real, listed[at], OFF * 512)
            put(i % PAIRS, jnp.where(real, OWN + at, SLOTS), (entry >> 9) & 511, entry & 511)
        return unused

    lax.fori_loop(0, (count + GROUP - 1) // GROUP, place_near, 0)

    for each in late:
        each.wait()

    def pixels(observed, background, image):
        e = jnp.exp(-jnp.abs(image))
        soft = jnp.maximum(image, 0.0) + jnp.log1p(e)
        sig = jnp.where(image >= 0.0, 1.0, e) / (1.0 + e)
        return (observed / (background + soft) - 1.0) * sig

    def images(row, rows):
        left = iota((rows, 128), 1) < 64

        def planes(parity):
            out = []
            for h in range(PLANES):
                at = pl.ds(h * CROWS + OFF + row, rows)
                plane = canvases[parity][at, :]
                for i in range(1, PAIRS):
                    plane = plane + canvases[2 * i + parity][at, :]
                out.append(plane)
            return out

        upper, lower = planes(0), planes(1)
        out = []
        for q in range(4):
            before = jnp.zeros((rows, 128), F32) if q == 0 else upper[2 * q - 1]
            image = upper[2 * q] + jnp.where(left, before, upper[2 * q + 1])
            before = jnp.zeros((rows, 128), F32) if q == 0 else lower[2 * q - 1]
            out.append(image + pltpu.roll(lower[2 * q] + jnp.where(left, lower[2 * q + 1], before), 64, 1))
        return out

    def reach(row, rows, values):
        values = [v.astype(BF16).astype(F32) for v in values]
        turned = [pltpu.roll(v, 64, 1) for v in values]
        left = iota((rows, 128), 1) < 64
        for q in range(4):
            after = min(q + 1, 3)
            even, odd = pl.ds(2 * q * XROWS + row, rows), pl.ds((2 * q + 1) * XROWS + row, rows)
            xs[even, :] = values[q]
            xs[odd, :] = jnp.where(left, values[after], values[q])
            xt[even, :] = turned[q]
            xt[odd, :] = jnp.where(left, turned[q], turned[after])

    def edge(from_first, row, real):
        values = []
        for q, image in enumerate(images(row, 32)):
            lanes = slice(q * 128, (q + 1) * 128)
            observed = jnp.where(from_first, first_ref[:32, lanes], second_ref[:32, lanes])
            background = jnp.where(from_first, first_ref[32:, lanes], second_ref[32:, lanes])
            values.append(jnp.where(real, pixels(observed, background, image), 0.0))
        reach(row, 32, values)

    even = (tile & 1) == 0
    edge(jnp.logical_not(even), 0, tile > 0)
    edge(even, 288, tile < NSKY - 1)

    def block(i, unused):
        base = pl.multiple_of(i * 32, 32)
        values = []
        for q, image in enumerate(images(32 + base, 32)):
            lanes = slice(q * 128, (q + 1) * 128)
            r = pixels(obs_ref[pl.ds(base, 32), lanes], back_ref[pl.ds(base, 32), lanes], image)
            res_ref[pl.ds(base, 32), lanes] = r
            values.append(r)
        reach(32 + base, 32, values)
        return unused

    lax.fori_loop(0, 8, block, 0, unroll=8)
    res_copy = pltpu.make_async_copy(res_ref, res_hbm, sems.at[2])
    res_copy.start()

    def window(g, unused):
        for i in range(CAP):
            row, col = row_s[g, i], col_s[g, i]
            turn = col & 127
            start = (col >> 6) * XROWS + row
            inside = ((lane32 - turn) & 127) < 64
            seen = jnp.where(inside, xs[pl.ds(start, 32), :], xt[pl.ds(start + 32, 32), :])
            ss[pl.ds(g * CAP + i, 32, stride=SROWS), :] = pltpu.roll(seen, (128 - turn) & 127, 1)
        return unused

    lax.fori_loop(0, NSKY, window, 0, unroll=8)

    total = jnp.zeros((OWN, 192), F32)
    for c in range(CHUNKS):
        base = 2 * c * SROWS
        w = jnp.concatenate([ss[base:base + OWN, :], ss[base + SROWS:base + SROWS + OWN, :]], axis=1).astype(BF16)
        total = total + dot(w, b_ref[c], ((1,), (1,)))
    grad = total[:, 128:192] + total[:, 64:128] + total[:, :64]
    grad = jnp.concatenate([grad, grad], axis=1)
    for o in range(NSKY):
        acc[o * 16:(o + 1) * 16, :] = jnp.where(k_at < count_s[0, o], grad[o * 16:(o + 1) * 16], 0.0)
    left = iota((4, 128), 1) < 64
    for o in range(NSKY):
        for ref, at in ((keep_ref, o * 16 + core * 8), (give_ref, o * 16 + 8 - core * 8)):
            ref[o] = jnp.where(left, acc[pl.ds(at, 4), :], acc[pl.ds(at + 4, 4), :])
    res_copy.wait()


def owner_kernel(first, second, got_ref, out_ref, sums):
    for t in range(NSKY):
        s = got_ref[t * 8]
        for z in range(1, 8):
            s = s + got_ref[t * 8 + z]
        sums[t * 4:(t + 1) * 4, :] = s
    x = sums[...]
    out = dot(x, first[...], ((0,), (0,)), HIGHEST)[:64] + dot(x, second[...], ((0,), (0,)), HIGHEST)[64:]
    out_ref[...] = out


SM = pl.BlockSpec(memory_space=pltpu.SMEM)
HB = pl.BlockSpec(memory_space=pltpu.HBM)
VM = pl.BlockSpec(memory_space=pltpu.VMEM)


def call_send(index, count, params_t, row, col):
    return pl.pallas_call(
        send_kernel,
        out_shape=jax.ShapeDtypeStruct((NSKY, 64, 128), BF16),
        in_specs=[SM, SM, VM, VM, VM],
        out_specs=VM,
        scratch_shapes=[pltpu.VMEM((256, 128), F32)],
        compiler_params=pltpu.CompilerParams(vmem_limit_bytes=60 << 20),
        cost_estimate=pl.CostEstimate(flops=8 * 10 ** 9, bytes_accessed=16 << 20, transcendentals=0),
    )(index, count, params_t, row, col)


def call_basis(index, taps, basis):
    return pl.pallas_call(
        basis_kernel,
        out_shape=(
            jax.ShapeDtypeStruct((CHUNKS, 192, 256), BF16),
            jax.ShapeDtypeStruct((64, 128), F32),
            jax.ShapeDtypeStruct((64, 128), F32),
        ),
        in_specs=[SM, VM, VM],
        out_specs=(HB, VM, VM),
        scratch_shapes=[
            pltpu.VMEM((8, 128), F32),
            pltpu.VMEM((33 * STEP, 128), F32),
            pltpu.VMEM((33 * STEP, 128), F32),
            pltpu.VMEM((CHUNKS, 192, 256), BF16),
            pltpu.SemaphoreType.DMA((4,)),
        ],
        compiler_params=pltpu.CompilerParams(vmem_limit_bytes=55_000_000),
        cost_estimate=pl.CostEstimate(flops=10 ** 5, bytes_accessed=1 << 10, transcendentals=0),
    )(index, taps, basis)


def call_sky(row, col, count, shaped, got, obs, back, first, second):
    return pl.pallas_call(
        sky_kernel,
        out_shape=(
            jax.ShapeDtypeStruct((TR, TW), F32),
            jax.ShapeDtypeStruct((NSKY, 4, 128), F32),
            jax.ShapeDtypeStruct((NSKY, 4, 128), F32),
        ),
        in_specs=[SM, SM, SM, HB, VM, HB, HB, VM, VM],
        out_specs=(HB, VM, VM),
        scratch_shapes=[
            pltpu.VMEM((CHUNKS, 192, 256), BF16),
            pltpu.VMEM((TR, TW), F32),
            pltpu.VMEM((TR, TW), F32),
            pltpu.VMEM((TR, TW), F32),
            pltpu.SemaphoreType.DMA((7,)),
            pltpu.VMEM((33 * SROWS, 128), F32),
            pltpu.VMEM((PLANES * XROWS, 128), F32),
            pltpu.VMEM((PLANES * XROWS, 128), F32),
            pltpu.VMEM((OWN, 128), F32),
            pltpu.VMEM((512, 128), F32),
            pltpu.VMEM((520, 128), F32),
            pltpu.VMEM((32, 128), jnp.int32),
            pltpu.SMEM((32, 128), jnp.int32),
            pltpu.SMEM((520,), jnp.int32),
            pltpu.SemaphoreType.DMA,
        ] + [pltpu.VMEM((PLANES * CROWS, 128), F32)] * (2 * PAIRS),
        compiler_params=pltpu.CompilerParams(vmem_limit_bytes=54_000_000),
        cost_estimate=pl.CostEstimate(flops=4 * 10 ** 9, bytes_accessed=4 << 20, transcendentals=0),
    )(row, col, count, shaped, got, obs, back, first, second)


def call_owner(first, second, got):
    return pl.pallas_call(
        owner_kernel,
        out_shape=jax.ShapeDtypeStruct((PS, 128), F32),
        in_specs=[VM, VM, VM],
        out_specs=VM,
        scratch_shapes=[pltpu.VMEM((64, 128), F32)],
        compiler_params=pltpu.CompilerParams(vmem_limit_bytes=8 << 20),
    )(first, second, got)


def on_device(params, basis, psf_taps, send_index, tile_count, stamp_row, stamp_col, observed, background):
    n = NSKY
    index = send_index[0]
    row, col = stamp_row[0], stamp_col[0]
    obs, back = observed[0], background[0]
    sent = call_send(index, tile_count, params.T, row, col)
    even = (lax.axis_index("sky") & 1) == 0
    low = jnp.concatenate([obs[TR - 32:], back[TR - 32:]], axis=0)
    high = jnp.concatenate([obs[:32], back[:32]], axis=0)
    first, second = jnp.where(even, low, high), jnp.where(even, high, low)
    got = lax.all_to_all(sent, "sky", split_axis=0, concat_axis=0, tiled=True)
    first = lax.ppermute(first, "sky", [(i, i ^ 1) for i in range(n)])
    second = lax.ppermute(second, "sky", [(i, ((i + 1) ^ 1) - 1) for i in range(1, n - 1)])
    shaped, hot_first, hot_second = call_basis(index, psf_taps[0], basis)
    residual, keep, give = call_sky(row, col, tile_count, shaped, got, obs, back, first, second)
    swap = [(i, i ^ 1) for i in range(16)]
    mine = keep + lax.ppermute(give, "epoch", swap)
    spread = jnp.broadcast_to(mine[:, None], (n, 8, 4, 128)).reshape(128, 4, 128)
    groups = [[t * 16 + z * 2 + c for t in range(16) for z in range(8)] for c in range(2)]
    back_home = lax.all_to_all(
        spread, ("sky", "epoch"), split_axis=0, concat_axis=0, tiled=True, axis_index_groups=groups
    )
    part = call_owner(hot_first, hot_second, back_home)
    grad = part + lax.ppermute(part, "epoch", swap)
    return grad.T, residual[None]


def solution(mesh):
    in_specs = (
        P("sky", None),
        P(),
        P("epoch", None, None),
        P("sky", None, None),
        P("sky", None),
        P("sky", None, None),
        P("sky", None, None),
        P("epoch", "sky", None),
        P("epoch", "sky", None),
    )
    out_specs = (P("sky", None), P("epoch", "sky", None))
    return jax.shard_map(on_device, mesh=mesh, in_specs=in_specs, out_specs=out_specs, check_vma=False)
```

```python
import jax
import jax.numpy as jnp
from jax import lax
from jax.experimental import pallas as pl
from jax.experimental.pallas import tpu as pltpu
from jax.sharding import PartitionSpec as P

PS = 64
TAPS = 51
HALF = 25
TR = 256
TW = 512
CAP = 16
NSKY = 16
OWN = 256
SLOTS = 768
SROWS = 776
OFF = 64
CROWS = 448
XROWS = 320
PLANES = 8
PAIRS = 2
GROUP = 32
CHUNKS = 16
BLOCK = 128
STEP = 72
DEAD = 128
HIGHEST = lax.Precision.HIGHEST
F32 = jnp.float32
BF16 = jnp.bfloat16


def dot(a, b, dims, precision=None):
    return lax.dot_general(a, b, (dims, ((), ())), precision=precision, preferred_element_type=F32)


def split3(x):
    high = x.astype(BF16)
    rest = x - high.astype(F32)
    mid = rest.astype(BF16)
    low = (rest - mid.astype(F32)).astype(BF16)
    return high, mid, low


def iota(shape, axis):
    return lax.broadcasted_iota(jnp.int32, shape, axis)


def send_kernel(index_s, count_s, params_ref, row_ref, col_ref, out_ref, hot):
    lane = iota((1, 128), 1)
    for t in range(NSKY):
        for k in range(CAP):
            hot[t * 16 + k:t * 16 + k + 1, :] = jnp.where(lane == index_s[t, k], 1.0, 0.0).astype(F32)
    rows = dot(hot[...].astype(BF16), params_ref[...], ((1,), (1,)))
    rows = jnp.concatenate([rows, rows], axis=1).astype(BF16)
    none = jnp.zeros((16, 128), BF16)
    owner, k_at = iota((NSKY, CAP), 0), iota((NSKY, CAP), 1)
    count = jnp.zeros((NSKY, CAP), jnp.int32)
    for o in range(NSKY):
        count = jnp.where(owner == o, count_s[0, o], count)
    row = jnp.where(k_at < count, row_ref[...], DEAD)
    col = col_ref[...]
    spots = jnp.concatenate([row, col >> 1, col & 1, jnp.zeros((NSKY, 80), jnp.int32)], axis=1)
    spots = spots.astype(F32).astype(BF16)
    for t in range(NSKY):
        mine = rows[t * 16:(t + 1) * 16]
        out_ref[t, 16:32, :] = mine
        if t + 1 < NSKY:
            out_ref[t + 1, 0:16, :] = mine
        if t > 0:
            out_ref[t - 1, 32:48, :] = mine
        out_ref[t, 48:64, :] = spots
    out_ref[0, 0:16, :] = none
    out_ref[NSKY - 1, 32:48, :] = none


def basis_kernel(index_s, taps_ref, basis_ref, out_hbm, first, second, taps_pad, xs, ts, out_ref, sems):
    core = lax.axis_index("epoch") & 1
    source = iota((1, 128), 1)
    for t in range(NSKY):
        for r in range(4):
            for hot, k in ((first, r), (second, r + 4)):
                hot[t * 4 + r:t * 4 + r + 1, :] = jnp.where(source == index_s[t, core * 8 + k], 1.0, 0.0).astype(F32)
    taps_pad[...] = jnp.zeros((8, 128), F32)
    taps = taps_ref[...]
    taps_pad[0:2, 0:TAPS] = taps / jnp.sum(taps, axis=1, keepdims=True)
    lane = iota((64, 128), 1)

    row_taps = jnp.broadcast_to(taps_pad[0:1, :], (32, 128))
    even = pltpu.roll(pltpu.roll(row_taps, 128 - HALF, 1), 0, 1, stride=2, stride_axis=0)
    odd = pltpu.roll(even, 1, 1)
    row_k = jnp.where(lane[:32] < 64, even, pltpu.roll(odd, 64, 1))
    rh, rm, rl = [x.astype(F32) for x in split3(row_k)]
    none = jnp.zeros((64, 128), F32)
    row_parts = jnp.concatenate([rl, rm, rh, rm, rh, rh, none], axis=0).T.astype(BF16)[:, :192]

    col_taps = jnp.broadcast_to(taps_pad[1:2, :], (64, 128))
    col_k = pltpu.roll(pltpu.roll(col_taps, 128 - HALF, 1), 0, 1, stride=1, stride_axis=0)
    col_k = jnp.concatenate([jnp.where(lane < 64, col_k, 0.0), jnp.where(lane < 64, 0.0, pltpu.roll(col_k, 64, 1))], axis=0)
    ch, cm, cl = split3(col_k)
    col_parts = jnp.concatenate([
        jnp.concatenate([ch, cm], axis=1), jnp.concatenate([cl, jnp.zeros((128, 128), BF16)], axis=1)], axis=0)

    for m in range(4):
        x = jnp.concatenate([basis_ref[:, j * 128:(j + 1) * 128] for j in range(m * 8, m * 8 + 8)], axis=0)
        made = dot(jnp.concatenate([x, x], axis=1), col_parts, ((1,), (0,)))
        made = made[:, :128] + made[:, 128:]
        for i in range(8):
            xs[(m * 8 + i) * STEP:(m * 8 + i) * STEP + 64, :] = made[i * 64:(i + 1) * 64]

    for g in range(8):
        wide = jnp.concatenate([xs[pl.ds(g * 8 + i, 32, stride=STEP), :] for i in range(8)], axis=1)
        wh, wm, wl = split3(wide)
        made = dot(row_parts, jnp.concatenate([wh, wm, wl, wh, wm, wh], axis=0), ((1,), (0,)))
        for i in range(8):
            both = jnp.where(lane < 64, made[:64, i * 128:(i + 1) * 128], made[64:, i * 128:(i + 1) * 128])
            both = both + pltpu.roll(both, 64, 1)
            ts[pl.ds(g * 8 + i, 32, stride=STEP), :] = jnp.where(lane[:32] < 64, both[:32], both[32:])

    copies = []
    for c in range(CHUNKS):
        y = jnp.concatenate([ts[pl.ds(2 * c * STEP, 64), :], ts[pl.ds((2 * c + 1) * STEP, 64), :]], axis=1)
        for part, v in enumerate(split3(y)):
            out_ref[c, part * 64:(part + 1) * 64, :] = v
        if c % 4 == 3:
            some = pl.ds(c - 3, 4)
            copies.append(pltpu.make_async_copy(out_ref.at[some], out_hbm.at[some], sems.at[c // 4]))
            copies[-1].start()
    for copy in copies:
        copy.wait()


def sky_kernel(row_s, col_s, count_s, b_hbm, got_ref, obs_hbm, back_hbm, first_ref, second_ref,
               res_hbm, keep_ref, give_ref, b_ref, obs_ref, back_ref, res_ref, sems, ss, xs, xt, acc, near, packed, spots_v, spots_s, listed, sem, *canvases):
    tile = lax.axis_index("sky")
    core = lax.axis_index("epoch") % 2
    lane32 = iota((32, 128), 1)

    def b_copy(i):
        some = pl.ds(4 * i, 4)
        return pltpu.make_async_copy(b_hbm.at[some], b_ref.at[some], sems.at[3 + i])

    for i in range(4):
        b_copy(i).start()
    late = [pltpu.make_async_copy(obs_hbm, obs_ref, sems.at[0]), pltpu.make_async_copy(back_hbm, back_ref, sems.at[1])]
    for each in late:
        each.start()

    slot_at = iota((NSKY, 128), 0) * 32 + iota((NSKY, 128), 1)

    def spots_of(peer, slot, shift, inside):
        spots = got_ref[peer, 48:64, :].astype(F32)
        row = spots.astype(jnp.int32)
        col = 2 * pltpu.roll(spots, 112, 1).astype(jnp.int32) + pltpu.roll(spots, 96, 1).astype(jnp.int32)
        return jnp.where(inside(row), (slot * 512 + row + shift) * 512 + col, -1)

    spots_v[0:16, :] = spots_of(
        jnp.maximum(tile - 1, 0), slot_at, OFF - TR, lambda row: (row > 192) & (tile > 0))
    spots_v[16:32, :] = spots_of(
        jnp.minimum(tile + 1, NSKY - 1), slot_at + 16, OFF + TR, lambda row: (row < 64) & (tile < NSKY - 1))
    copy = pltpu.make_async_copy(spots_v, spots_s, sem)
    copy.start()

    k_at = iota((CAP, 128), 0)
    mine = []
    for o in range(NSKY):
        mine.append(jnp.where(k_at < count_s[0, o], got_ref[o, 16:32, :].astype(F32), 0.0).astype(BF16))
        near[o * 32:o * 32 + 16, :] = got_ref[o, 0:16, :].astype(F32)
        near[o * 32 + 16:o * 32 + 32, :] = got_ref[o, 32:48, :].astype(F32)

    def three(x):
        return jnp.concatenate([x, x[:, :64]], axis=1)

    mine = three(jnp.concatenate(mine, axis=0))
    for j in range(32):
        ss[j * SROWS + SLOTS:(j + 1) * SROWS, :] = jnp.zeros((SROWS - SLOTS, 128), F32)
    copy.wait()

    span = PLANES * CROWS // CHUNKS

    def render(c, count):
        made = dot(mine, b_ref[c], ((1,), (0,)))
        made = made.astype(BF16).astype(F32)
        base = pl.multiple_of(c * (2 * SROWS), 8)
        ss[pl.ds(base, OWN), :] = made[:, :128]
        ss[pl.ds(base + SROWS, OWN), :] = made[:, 128:]
        for canvas in canvases:
            canvas[pl.ds(pl.multiple_of(c * span, 8), span), :] = jnp.zeros((span, 128), F32)
        for which in range(2):
            for k in range(CAP):
                entry = spots_s[which * 16 + c, k]
                listed[count] = entry
                count = count + jnp.where(entry >= 0, 1, 0)
        return count

    count = tile * 0
    for i in range(4):
        b_copy(i).wait()
        count = lax.fori_loop(4 * i, 4 * i + 4, render, count, unroll=4)

    def pack(g, unused):
        for i in range(GROUP):
            at = g * GROUP + i
            entry = jnp.where(at < count, listed[at], 0)
            packed[pl.ds(at, 1), :] = near[pl.ds(entry >> 18, 1), :]
        return unused

    lax.fori_loop(0, (count + GROUP - 1) // GROUP, pack, 0)

    def render_near(b, unused):
        base = pl.multiple_of(b * BLOCK, BLOCK)
        x = three(packed[pl.ds(base, BLOCK), :].astype(BF16))
        for c in range(CHUNKS):
            made = dot(x, b_ref[c], ((1,), (0,))).astype(BF16).astype(F32)
            ss[pl.ds(2 * c * SROWS + OWN + base, BLOCK), :] = made[:, :128]
            ss[pl.ds((2 * c + 1) * SROWS + OWN + base, BLOCK), :] = made[:, 128:]
        return unused

    lax.fori_loop(0, (count + BLOCK - 1) // BLOCK, render_near, 0)

    def put(i, slot, row, col):
        turn = col & 127
        start = (col >> 6) * CROWS + row
        turned = pltpu.roll(ss[pl.ds(slot, 32, stride=SROWS), :], turn, 1)
        inside = ((lane32 - turn) & 127) < 64
        canvases[2 * i][pl.ds(start, 32), :] += jnp.where(inside, turned, 0.0)
        canvases[2 * i + 1][pl.ds(start + 32, 32), :] += jnp.where(inside, 0.0, turned)

    def place(g, unused):
        for i in range(CAP):
            put(i % PAIRS, g * CAP + i, row_s[g, i] + OFF, col_s[g, i])
        return unused

    lax.fori_loop(0, NSKY, place, 0, unroll=16)

    def place_near(g, unused):
        for i in range(GROUP):
            at = g * GROUP + i
            real = at < count
            entry = jnp.where(real, listed[at], OFF * 512)
            put(i % PAIRS, jnp.where(real, OWN + at, SLOTS), (entry >> 9) & 511, entry & 511)
        return unused

    lax.fori_loop(0, (count + GROUP - 1) // GROUP, place_near, 0)

    for each in late:
        each.wait()

    def pixels(observed, background, image):
        e = jnp.exp(-jnp.abs(image))
        soft = jnp.maximum(image, 0.0) + jnp.log1p(e)
        sig = jnp.where(image >= 0.0, 1.0, e) / (1.0 + e)
        return (observed / (background + soft) - 1.0) * sig

    def images(row, rows):
        left = iota((rows, 128), 1) < 64

        def planes(parity):
            out = []
            for h in range(PLANES):
                at = pl.ds(h * CROWS + OFF + row, rows)
                plane = canvases[parity][at, :]
                for i in range(1, PAIRS):
                    plane = plane + canvases[2 * i + parity][at, :]
                out.append(plane)
            return out

        upper, lower = planes(0), planes(1)
        out = []
        for q in range(4):
            before = jnp.zeros((rows, 128), F32) if q == 0 else upper[2 * q - 1]
            image = upper[2 * q] + jnp.where(left, before, upper[2 * q + 1])
            before = jnp.zeros((rows, 128), F32) if q == 0 else lower[2 * q - 1]
            out.append(image + pltpu.roll(lower[2 * q] + jnp.where(left, lower[2 * q + 1], before), 64, 1))
        return out

    def reach(row, rows, values):
        values = [v.astype(BF16).astype(F32) for v in values]
        turned = [pltpu.roll(v, 64, 1) for v in values]
        left = iota((rows, 128), 1) < 64
        for q in range(4):
            after = min(q + 1, 3)
            even, odd = pl.ds(2 * q * XROWS + row, rows), pl.ds((2 * q + 1) * XROWS + row, rows)
            xs[even, :] = values[q]
            xs[odd, :] = jnp.where(left, values[after], values[q])
            xt[even, :] = turned[q]
            xt[odd, :] = jnp.where(left, turned[q], turned[after])

    def edge(from_first, row, real):
        values = []
        for q, image in enumerate(images(row, 32)):
            lanes = slice(q * 128, (q + 1) * 128)
            observed = jnp.where(from_first, first_ref[:32, lanes], second_ref[:32, lanes])
            background = jnp.where(from_first, first_ref[32:, lanes], second_ref[32:, lanes])
            values.append(jnp.where(real, pixels(observed, background, image), 0.0))
        reach(row, 32, values)

    even = (tile & 1) == 0
    edge(jnp.logical_not(even), 0, tile > 0)
    edge(even, 288, tile < NSKY - 1)

    def block(i, unused):
        base = pl.multiple_of(i * 32, 32)
        values = []
        for q, image in enumerate(images(32 + base, 32)):
            lanes = slice(q * 128, (q + 1) * 128)
            r = pixels(obs_ref[pl.ds(base, 32), lanes], back_ref[pl.ds(base, 32), lanes], image)
            res_ref[pl.ds(base, 32), lanes] = r
            values.append(r)
        reach(32 + base, 32, values)
        return unused

    lax.fori_loop(0, 8, block, 0, unroll=8)
    res_copy = pltpu.make_async_copy(res_ref, res_hbm, sems.at[2])
    res_copy.start()

    def window(g, unused):
        for i in range(CAP):
            row, col = row_s[g, i], col_s[g, i]
            turn = col & 127
            start = (col >> 6) * XROWS + row
            inside = ((lane32 - turn) & 127) < 64
            seen = jnp.where(inside, xs[pl.ds(start, 32), :], xt[pl.ds(start + 32, 32), :])
            ss[pl.ds(g * CAP + i, 32, stride=SROWS), :] = pltpu.roll(seen, (128 - turn) & 127, 1)
        return unused

    lax.fori_loop(0, NSKY, window, 0, unroll=8)

    total = jnp.zeros((OWN, 192), F32)
    for c in range(CHUNKS):
        base = 2 * c * SROWS
        w = jnp.concatenate([ss[base:base + OWN, :], ss[base + SROWS:base + SROWS + OWN, :]], axis=1).astype(BF16)
        total = total + dot(w, b_ref[c], ((1,), (1,)))
    grad = total[:, 128:192] + total[:, 64:128] + total[:, :64]
    grad = jnp.concatenate([grad, grad], axis=1)
    for o in range(NSKY):
        acc[o * 16:(o + 1) * 16, :] = jnp.where(k_at < count_s[0, o], grad[o * 16:(o + 1) * 16], 0.0)
    left = iota((4, 128), 1) < 64
    for o in range(NSKY):
        for ref, at in ((keep_ref, o * 16 + core * 8), (give_ref, o * 16 + 8 - core * 8)):
            ref[o] = jnp.where(left, acc[pl.ds(at, 4), :], acc[pl.ds(at + 4, 4), :])
    res_copy.wait()


def owner_kernel(first, second, got_ref, out_ref, sums):
    for t in range(NSKY):
        s = got_ref[t * 8]
        for z in range(1, 8):
            s = s + got_ref[t * 8 + z]
        sums[t * 4:(t + 1) * 4, :] = s
    x = sums[...]
    out = dot(x, first[...], ((0,), (0,)), HIGHEST)[:64] + dot(x, second[...], ((0,), (0,)), HIGHEST)[64:]
    out_ref[...] = out


SM = pl.BlockSpec(memory_space=pltpu.SMEM)
HB = pl.BlockSpec(memory_space=pltpu.HBM)
VM = pl.BlockSpec(memory_space=pltpu.VMEM)


def call_send(index, count, params_t, row, col):
    return pl.pallas_call(
        send_kernel,
        out_shape=jax.ShapeDtypeStruct((NSKY, 64, 128), BF16),
        in_specs=[SM, SM, VM, VM, VM],
        out_specs=VM,
        scratch_shapes=[pltpu.VMEM((256, 128), F32)],
        compiler_params=pltpu.CompilerParams(vmem_limit_bytes=60 << 20),
        cost_estimate=pl.CostEstimate(flops=8 * 10 ** 9, bytes_accessed=16 << 20, transcendentals=0),
    )(index, count, params_t, row, col)


def call_basis(index, taps, basis):
    return pl.pallas_call(
        basis_kernel,
        out_shape=(
            jax.ShapeDtypeStruct((CHUNKS, 192, 256), BF16),
            jax.ShapeDtypeStruct((64, 128), F32),
            jax.ShapeDtypeStruct((64, 128), F32),
        ),
        in_specs=[SM, VM, VM],
        out_specs=(HB, VM, VM),
        scratch_shapes=[
            pltpu.VMEM((8, 128), F32),
            pltpu.VMEM((33 * STEP, 128), F32),
            pltpu.VMEM((33 * STEP, 128), F32),
            pltpu.VMEM((CHUNKS, 192, 256), BF16),
            pltpu.SemaphoreType.DMA((4,)),
        ],
        compiler_params=pltpu.CompilerParams(vmem_limit_bytes=55_000_000),
        cost_estimate=pl.CostEstimate(flops=10 ** 5, bytes_accessed=1 << 10, transcendentals=0),
    )(index, taps, basis)


def call_sky(row, col, count, shaped, got, obs, back, first, second):
    return pl.pallas_call(
        sky_kernel,
        out_shape=(
            jax.ShapeDtypeStruct((TR, TW), F32),
            jax.ShapeDtypeStruct((NSKY, 4, 128), F32),
            jax.ShapeDtypeStruct((NSKY, 4, 128), F32),
        ),
        in_specs=[SM, SM, SM, HB, VM, HB, HB, VM, VM],
        out_specs=(HB, VM, VM),
        scratch_shapes=[
            pltpu.VMEM((CHUNKS, 192, 256), BF16),
            pltpu.VMEM((TR, TW), F32),
            pltpu.VMEM((TR, TW), F32),
            pltpu.VMEM((TR, TW), F32),
            pltpu.SemaphoreType.DMA((7,)),
            pltpu.VMEM((33 * SROWS, 128), F32),
            pltpu.VMEM((PLANES * XROWS, 128), F32),
            pltpu.VMEM((PLANES * XROWS, 128), F32),
            pltpu.VMEM((OWN, 128), F32),
            pltpu.VMEM((512, 128), F32),
            pltpu.VMEM((520, 128), F32),
            pltpu.VMEM((32, 128), jnp.int32),
            pltpu.SMEM((32, 128), jnp.int32),
            pltpu.SMEM((520,), jnp.int32),
            pltpu.SemaphoreType.DMA,
        ] + [pltpu.VMEM((PLANES * CROWS, 128), F32)] * (2 * PAIRS),
        compiler_params=pltpu.CompilerParams(vmem_limit_bytes=54_000_000),
        cost_estimate=pl.CostEstimate(flops=4 * 10 ** 9, bytes_accessed=4 << 20, transcendentals=0),
    )(row, col, count, shaped, got, obs, back, first, second)


def call_owner(first, second, got):
    return pl.pallas_call(
        owner_kernel,
        out_shape=jax.ShapeDtypeStruct((PS, 128), F32),
        in_specs=[VM, VM, VM],
        out_specs=VM,
        scratch_shapes=[pltpu.VMEM((64, 128), F32)],
        compiler_params=pltpu.CompilerParams(vmem_limit_bytes=8 << 20),
    )(first, second, got)


def on_device(params, basis, psf_taps, send_index, tile_count, stamp_row, stamp_col, observed, background):
    n = NSKY
    index = send_index[0]
    row, col = stamp_row[0], stamp_col[0]
    obs, back = observed[0], background[0]
    sent = call_send(index, tile_count, params.T, row, col)
    even = (lax.axis_index("sky") & 1) == 0
    low = jnp.concatenate([obs[TR - 32:], back[TR - 32:]], axis=0)
    high = jnp.concatenate([obs[:32], back[:32]], axis=0)
    first, second = jnp.where(even, low, high), jnp.where(even, high, low)
    got = lax.all_to_all(sent, "sky", split_axis=0, concat_axis=0, tiled=True)
    first = lax.ppermute(first, "sky", [(i, i ^ 1) for i in range(n)])
    second = lax.ppermute(second, "sky", [(i, ((i + 1) ^ 1) - 1) for i in range(1, n - 1)])
    shaped, hot_first, hot_second = call_basis(index, psf_taps[0], basis)
    residual, keep, give = call_sky(row, col, tile_count, shaped, got, obs, back, first, second)
    swap = [(i, i ^ 1) for i in range(16)]
    mine = keep + lax.ppermute(give, "epoch", swap)
    spread = jnp.broadcast_to(mine[:, None], (n, 8, 4, 128)).reshape(128, 4, 128)
    groups = [[t * 16 + z * 2 + c for t in range(16) for z in range(8)] for c in range(2)]
    back_home = lax.all_to_all(
        spread, ("sky", "epoch"), split_axis=0, concat_axis=0, tiled=True, axis_index_groups=groups
    )
    part = call_owner(hot_first, hot_second, back_home)
    grad = part + lax.ppermute(part, "epoch", swap)
    return grad.T, residual[None]


def solution(mesh):
    in_specs = (
        P("sky", None),
        P(),
        P("epoch", None, None),
        P("sky", None, None),
        P("sky", None),
        P("sky", None, None),
        P("sky", None, None),
        P("epoch", "sky", None),
        P("epoch", "sky", None),
    )
    out_specs = (P("sky", None), P("epoch", "sky", None))
    return jax.shard_map(on_device, mesh=mesh, in_specs=in_specs, out_specs=out_specs, check_vma=False)
```
